512 devices in a mesh: row: 32 (over y, z_lo, core), col: 16 (over x, z_hi).
Axes of the slice: x: 4, y: 8, z: 8 (z_hi: 4, z_lo: 2; z = z_hi * 2 + z_lo), core: 2. Of those that a mesh axis runs over, the one named last changes fastest.
Arguments:
- start_amps: float32 [4096, 4096], P('row', 'col'), may hold values from -1.75 to 1.75
- exchange_ints: bfloat16 [4096, 4096], P('row', 'col'), may hold values from -6 to 6
- fitted_ints: bfloat16 [4096, 24576], P('col', 'row'), may hold values from -0.25 to 0.25
- pao_energy: float32 [2048], replicated, may hold values from 0.3 to 3
- occ_fock: float32 [8, 8], replicated, may hold values from -1.5 to 0.6, as said below
- domains: int32 [8, 512], replicated, may hold values from 0 to 2047, as said below
- pair_list: int32 [36, 2], replicated, may hold values from 0 to 7, as said below
Outputs:
- sym_amps: float32 [4096, 4096], P('row', 'col')
- gamma: bfloat16 [4096, 24576], P('col', 'row')
The draws below stay inside these ranges and needn't reach their ends.
Inputs may be any that keep to these rules, and one draw needn't show every extreme that they name: `pair_list`: each row is an ordered pair (I, J) of orbitals. Every (I, I) is listed; when (I, J) is listed so is (J, I); no pair is listed twice; 14 unordered pairs of distinct orbitals are listed. `domains`: each row holds 512 distinct PAO indices. `occ_fock`: Symmetric; its diagonal lies between -1.5 and -0.4.
All inputs are finite; a program needn't handle non-finite values.
Results may differ from the reference program's by a relative error of at most 0.001.
The reference program's roundings to bfloat16 on the way count: a program that leaves them out, or rounds other values in their place, can miss the bound.
Values may be sent and summed in bfloat16 or wider, within the bound.
A program may use at most 64 MiB of HBM per device.

```python
import math
import jax
import jax.numpy as jnp
from jax import lax

NOCC = 8
DOM = 512
NPAO = 2048
ITERS = 2
NKEEP = 14
NPAIR = 36
SPACE = 4096
NAUX = 24576


def draw_occ_fock(key, part):
    key = jax.random.fold_in(key, 11)
    diag_key, off_key = jax.random.split(key)
    diagonal = -jax.random.uniform(diag_key, (NOCC,), jnp.float32, 0.4, 1.5)
    rough = 0.2 * jnp.clip(jax.random.normal(off_key, (NOCC, NOCC), jnp.float32), -3.0, 3.0)
    coupling = 0.5 * (rough + rough.T)
    identity = jnp.eye(NOCC, dtype=jnp.float32)
    return coupling * (1.0 - identity) + diagonal[:, None] * identity


def draw_domains(key, part):
    key = jax.random.fold_in(key, 23)
    start_key, order_key = jax.random.split(key)
    starts = jax.random.randint(start_key, (NOCC,), 0, NPAO - DOM + 1)
    orbits = jnp.arange(NOCC)
    starts = jnp.where(orbits == 0, 0, jnp.where(orbits == NOCC - 1, NPAO - DOM, starts))
    order_keys = jax.random.split(order_key, NOCC)
    shuffled = jax.vmap(lambda single: jax.random.permutation(single, DOM))(order_keys)
    return (starts[:, None] + shuffled).astype(jnp.int32)


def draw_pair_list(key, part):
    key = jax.random.fold_in(key, 37)
    choose_key, order_key = jax.random.split(key)
    upper_first, upper_second = jnp.triu_indices(NOCC, 1)
    chosen = jax.random.permutation(choose_key, upper_first.shape[0])[:NKEEP]
    kept_first = upper_first[chosen]
    kept_second = upper_second[chosen]
    orbits = jnp.arange(NOCC)
    first_col = jnp.concatenate([orbits, kept_first, kept_second])
    second_col = jnp.concatenate([orbits, kept_second, kept_first])
    listing = jnp.stack([first_col, second_col], axis=1).astype(jnp.int32)
    shuffle = jax.random.permutation(order_key, NPAIR)
    return listing[shuffle]


def level_of(own_key, dims, pieces, low, largest):
    gain, own = 1.0, jax.random.fold_in(own_key, 6)
    for dim, shards_of in pieces:
        draws = jnp.exp(jax.random.uniform(jax.random.fold_in(own, dim), (shards_of,), jnp.float32, low / len(pieces), largest / len(pieces)))
        gain = gain * jnp.repeat(draws, dims[dim] // shards_of).reshape([-1 if axis == dim else 1 for axis in range(len(dims))])
    return gain


def bell_draw(stream_key, shape, scale, most, cuts=(), kind=jnp.bfloat16):
    entries = scale * jax.random.normal(stream_key, shape, jnp.float32)
    if cuts:
        entries = entries * level_of(stream_key, shape, cuts, -0.22, 0.18)
    return jnp.clip(entries, -most, most).astype(kind)


def setup_inputs(seed: int = 0) -> dict:
    keys = jax.random.split(jax.random.key(seed), 8)
    return {
        "start_amps": bell_draw(keys[0], (SPACE, SPACE), 0.3, 1.75, ((0, 32), (1, 16)), jnp.float32),
        "exchange_ints": bell_draw(keys[1], (SPACE, SPACE), 1.0, 6.0, ((0, 32), (1, 16))),
        "fitted_ints": bell_draw(keys[2], (SPACE, NAUX), (SPACE // 8) ** -0.5, 0.25, ((0, 16), (1, 32))),
        "pao_energy": jnp.clip(jnp.exp(jax.random.uniform(keys[3], (NPAO,), jnp.float32, math.log(0.3), math.log(3.0))), 0.3, 3.0),
        "occ_fock": draw_occ_fock(jax.random.fold_in(keys[7], 71), 0),
        "domains": draw_domains(jax.random.fold_in(keys[7], 71), 0),
        "pair_list": draw_pair_list(jax.random.fold_in(keys[7], 71), 0),
    }


full_precision = lax.Precision.HIGHEST


def lookup(values_table, indices):
    extent = values_table.shape[0]
    matches = indices[:, None] == jnp.arange(extent, dtype=jnp.int32)[None, :]
    return jnp.sum(jnp.where(matches, values_table[None, :], 0.0), axis=1)


def pair_mask(pair_list, norbit):
    orbits = jnp.arange(norbit, dtype=jnp.int32)
    first_hot = (pair_list[:, 0][:, None] == orbits[None, :]).astype(jnp.float32)
    second_hot = (pair_list[:, 1][:, None] == orbits[None, :]).astype(jnp.float32)
    return jnp.dot(first_hot.T, second_hot, precision=full_precision)


def placement(paos, domains, owners, fock_rows):
    norbit, width = domains.shape
    matches = paos[:, None, None] == domains[None, :, :]
    where_at = jnp.sum(jnp.where(matches, jnp.arange(width, dtype=jnp.int32)[None, None, :], 0), axis=2)
    present = jnp.any(matches, axis=2)
    orbits = jnp.arange(norbit, dtype=jnp.int32)
    position = (orbits[None, :] * width + where_at).astype(jnp.int32)
    weight = jnp.where(present & (owners[:, None] != orbits[None, :]), fock_rows, 0.0)
    return position, weight


def reference(start_amps, exchange_ints, fitted_ints, pao_energy, occ_fock, domains, pair_list):
    norbit, width = domains.shape
    extent = norbit * width
    listed = pair_mask(pair_list, norbit)
    owners = jnp.arange(extent, dtype=jnp.int32) // width
    orbits = jnp.arange(norbit, dtype=jnp.int32)
    picker = (owners[:, None] == orbits[None, :]).astype(jnp.float32)
    flat_domains = domains.reshape(-1)
    level = lookup(pao_energy, flat_domains) - jnp.dot(picker, jnp.diagonal(occ_fock), precision=full_precision)
    denominator = level[:, None] + level[None, :]
    full_mask = jnp.dot(jnp.dot(picker, listed, precision=full_precision), picker.T, precision=full_precision)
    position, weight = placement(flat_domains, domains, owners, jnp.dot(picker, occ_fock, precision=full_precision))
    exchange_full = exchange_ints.astype(jnp.float32)
    current = start_amps
    for sweep in range(ITERS):
        rounded = current.astype(jnp.bfloat16)
        left_term = jnp.zeros((extent, extent), jnp.float32)
        right_term = jnp.zeros((extent, extent), jnp.float32)
        for orbital in range(norbit):
            rows_taken = jnp.take(rounded, position[:, orbital], axis=0).astype(jnp.float32)
            left_term = left_term + weight[:, orbital][:, None] * rows_taken
            cols_taken = jnp.take(rounded, position[:, orbital], axis=1).astype(jnp.float32)
            right_term = right_term + cols_taken * weight[:, orbital][None, :]
        current = full_mask * ((left_term + right_term - exchange_full) / denominator)
    sym_amps = 0.5 * (current + current.T)
    gamma = jnp.dot(sym_amps.astype(jnp.bfloat16), fitted_ints, preferred_element_type=jnp.float32)
    return sym_amps, gamma.astype(jnp.bfloat16)
```

```python
import jax
import jax.numpy as jnp
from jax import lax
from jax.experimental import pallas as pl
from jax.experimental.pallas import tpu as pltpu
from jax.sharding import PartitionSpec as P

ITERS = 2
MESH = pl.DeviceIdType.MESH
F32 = jnp.float32
BF16 = jnp.bfloat16
ROWS, COLS, DOM, NORB = 128, 256, 512, 8
NY, NX, NZ = 8, 4, 4
FIRST_ROWS = 192
MAX_COPIES = 128


def turn(place, by, count):
    return lax.rem(place + (by + count), count)


def kernel(
    amps, exch, fitted, scal, dom, dom_cols, own_row_dom, own_col_dom, row_level, col_level,
    sym_out, gamma_out,
    fit_all, left_all, right_all, left_part, left_sib, left_zsend, left_zrecv, right_part,
    right_recv, left_hot, right_hot, mir_send, mir_recv, sym_all, acc, send_sems, recv_sems, own_sem,
):
    row = lax.axis_index("row")
    col = lax.axis_index("col")
    y, quarter = row // 4, lax.rem(row, 4)
    zl, core = quarter // 2, lax.rem(quarter, 2)
    x, zh = col // 4, lax.rem(col, 4)
    b2, half = zh // 2, lax.rem(zh, 2)
    orb = col // 2

    def device(y_=y, zl_=zl, core_=core, x_=x, zh_=zh):
        return {"row": y_ * 4 + zl_ * 2 + core_, "col": x_ * 4 + zh_}

    y_up, y_down = device(y_=turn(y, 1, NY)), device(y_=turn(y, -1, NY))
    x_up, x_down = device(x_=turn(x, 1, NX)), device(x_=turn(x, -1, NX))
    z_up, z_down = device(zh_=turn(zh, 1, NZ)), device(zh_=turn(zh, -1, NZ))
    z_far = device(zh_=turn(zh, 2, NZ))
    z_pair = device(zl_=1 - zl)
    sibling = device(core_=1 - core)
    half_pair = device(zh_=b2 * 2 + 1 - half)
    diagonal = row // 2 == col
    mirror = [
        {"row": col * 2 + t, "col": row // 2} for t in range(2)
    ]
    mine = [jnp.logical_and(diagonal, core == t) for t in range(2)]

    barrier = pltpu.get_barrier_semaphore()
    partners = [y_up, y_down, x_up, x_down, z_up, z_down, z_far, z_pair, sibling]
    for partner in partners:
        pl.semaphore_signal(barrier, inc=1, device_id=partner, device_id_type=MESH)
    for t in range(2):

        @pl.when(jnp.logical_not(mine[t]))
        def _():
            pl.semaphore_signal(barrier, inc=1, device_id=mirror[t], device_id_type=MESH)

    pl.semaphore_wait(barrier, len(partners) + 2 - diagonal.astype(jnp.int32))

    sent = []
    sites = [0]

    def send(src, dst, target):
        site = sites[0]
        sites[0] += 1
        copy = pltpu.make_async_remote_copy(
            src_ref=src, dst_ref=dst, send_sem=send_sems.at[site], recv_sem=recv_sems.at[site],
            device_id=target, device_id_type=MESH,
        )
        copy.start()
        sent.append(copy)
        return copy

    def fit_gather(low, count, first_is_z):
        if first_is_z:
            one, two, n = zh, x, NZ
            one_up, one_down, two_up, two_down = z_up, z_down, x_up, x_down
            slot = lambda i, j: j * 4 + i
        else:
            one, two, n = x, zh, NX
            one_up, one_down, two_up, two_down = x_up, x_down, z_up, z_down
            slot = lambda i, j: i * 4 + j

        def at(i, j, piece=None):
            if piece is None:
                return fit_all.at[slot(i, j), pl.ds(low, count), :]
            return fit_all.at[slot(i, j), pl.ds(low + piece * (count // 2), count // 2), :]

        offsets = (0, -1, 1, 2)
        held = {}
        state = {}

        def along_two(d, src=None):
            i = turn(one, d, n)
            src = at(i, two) if src is None else src
            held[d] = (send(src, at(i, two), two_up), send(src, at(i, two), two_down))

        def start():
            own = fitted.at[pl.ds(low, count), :]
            state["up"] = send(own, at(one, two), one_up)
            state["down"] = send(own, at(one, two), one_down)
            along_two(0, own)

        def step_one():
            state["up"].wait_recv()
            i = turn(one, -1, n)
            state["far_up"] = send(at(i, two, 0), at(i, two, 0), one_up)
            along_two(-1)
            state["down"].wait_recv()
            i = turn(one, 1, n)
            state["far_down"] = send(at(i, two, 1), at(i, two, 1), one_down)
            along_two(1)

        def step_two():
            state["far_up"].wait_recv()
            state["far_down"].wait_recv()
            along_two(2)

        far = {}

        def step_three(d):
            up, down = held[d]
            i = turn(one, d, n)
            up.wait_recv()
            j = turn(two, -1, n)
            first = send(at(i, j, 0), at(i, j, 0), two_up)
            down.wait_recv()
            j = turn(two, 1, n)
            far[d] = (first, send(at(i, j, 1), at(i, j, 1), two_down))

        def step_four():
            for d in offsets:
                for copy in far[d]:
                    copy.wait_recv()

        return start, step_one, step_two, step_three, step_four

    fit_a = fit_gather(0, FIRST_ROWS, True)
    fit_b = fit_gather(FIRST_ROWS, COLS - FIRST_ROWS, False)
    own_fit = pltpu.make_async_copy(fitted, fit_all.at[col], own_sem)

    def build_hots():
        for k in range(NORB):
            picked = dom[k : k + 1, pl.ds(pl.multiple_of(quarter * ROWS, ROWS), ROWS)]
            left_hot[k] = jnp.where(own_row_dom[...] == picked, 1.0, 0.0).astype(BF16)
            picked = dom_cols[pl.ds(pl.multiple_of(half * COLS, COLS), COLS), k : k + 1]
            right_hot[k] = jnp.where(picked == own_col_dom[...], 1.0, 0.0).astype(BF16)

    def iteration(t, current, hooks):
        rounded = current.astype(BF16)
        left_all[t, y] = rounded
        right_all[t, orb] = rounded
        lefts, rights = left_all.at[t], right_all.at[t]
        far = send(rights.at[orb], rights.at[orb], z_far)
        up = send(lefts.at[y], lefts.at[y], y_up)
        down = send(lefts.at[y], lefts.at[y], y_down)
        x_one = (
            send(rights.at[orb], rights.at[orb], x_up),
            send(rights.at[orb], rights.at[orb], x_down),
        )
        hooks[0]()
        left_part[t] = jnp.zeros((2, 2, ROWS, COLS), F32)
        right_part[t] = jnp.zeros((2, ROWS, COLS), F32)

        def left_add(k):
            term = jnp.dot(left_hot[k], left_all[t, k], preferred_element_type=F32) * scal[k]
            left_part[t] += term.reshape(2, 2, ROWS, COLS)

        def right_add(k):
            term = jnp.dot(right_all[t, k], right_hot[k], preferred_element_type=F32) * scal[NORB + k]
            right_part[t, 0] += term[:, :COLS]
            right_part[t, 1] += term[:, COLS:]

        other = x * 2 + 1 - b2
        far.wait_recv()
        x_two = (
            send(rights.at[other], rights.at[other], x_up),
            send(rights.at[other], rights.at[other], x_down),
        )

        def y_step(distance, up, down):
            up.wait_recv()
            below = turn(y, -distance, NY)
            down.wait_recv()
            above = turn(y, distance, NY)
            if distance < 3:
                up = send(lefts.at[below], lefts.at[below], y_up)
                down = send(lefts.at[above], lefts.at[above], y_down)
            else:
                low, high = pl.ds(0, ROWS // 2), pl.ds(ROWS // 2, ROWS // 2)
                up = send(lefts.at[below, low], lefts.at[below, low], y_up)
                down = send(lefts.at[above, high], lefts.at[above, high], y_down)
            return below, above, up, down

        def x_step(copies, bit):
            low, high = pl.ds(0, ROWS // 2), pl.ds(ROWS // 2, ROWS // 2)
            copies[0].wait_recv()
            below = turn(x, -1, NX) * 2 + bit
            up = send(rights.at[below, low], rights.at[below, low], x_up)
            copies[1].wait_recv()
            above = turn(x, 1, NX) * 2 + bit
            down = send(rights.at[above, high], rights.at[above, high], x_down)
            return below, above, up, down

        below, above, up, down = y_step(1, up, down)
        x_below, x_above, far_up_one, far_down_one = x_step(x_one, b2)
        right_add(other)
        left_add(below)
        left_add(above)
        below, above, up, down = y_step(2, up, down)
        x_below_two, x_above_two, far_up_two, far_down_two = x_step(x_two, 1 - b2)
        right_add(x_below)
        right_add(x_above)
        left_add(below)
        left_add(above)
        below, above, up, down = y_step(3, up, down)
        right_add(x_below_two)
        right_add(x_above_two)
        left_add(below)
        left_add(above)
        across = turn(x, 2, NX) * 2
        far_up_one.wait_recv()
        far_down_one.wait_recv()
        right_add(across + b2)
        far_up_two.wait_recv()
        far_down_two.wait_recv()
        right_add(across + 1 - b2)
        right_copy = send(right_part.at[t, 1 - half], right_recv.at[t], half_pair)
        up.wait_recv()
        down.wait_recv()
        left_add(turn(y, 4, NY))
        sib_copy = send(left_part.at[t, 1 - core], left_sib.at[t], sibling)
        hooks[1]()
        sib_copy.wait_recv()
        left_zsend[t] = left_part[t, core, 1 - zl] + left_sib[t, 1 - zl]
        z_copy = send(left_zsend.at[t], left_zrecv.at[t], z_pair)
        hooks[2]()
        right_copy.wait_recv()
        right_term = right_part[t, half] + right_recv[t]
        z_copy.wait_recv()
        left_term = left_part[t, core, zl] + left_sib[t, zl] + left_zrecv[t]
        denominator = row_level[...] + col_level[...]
        return scal[2 * NORB] * ((left_term + right_term - exch[...].astype(F32)) / denominator)

    def start_fitted():
        fit_a[0]()
        fit_b[0]()
        own_fit.start()
        build_hots()

    def nothing():
        pass

    def fit_one():
        fit_b[1]()
        fit_a[1]()

    def fit_two():
        fit_b[2]()
        fit_a[2]()

    current = iteration(0, amps[...], (start_fitted, nothing, nothing))
    fit_one()
    current = iteration(1, current, (nothing, nothing, fit_two))

    mir_sites = sites[0]
    sites[0] += 2
    mir_copies = []
    for t in range(2):
        mir_send[t] = current[:, t * ROWS : (t + 1) * ROWS].T
        mir_copies.append(
            pltpu.make_async_remote_copy(
                src_ref=mir_send.at[t], dst_ref=mir_recv.at[core],
                send_sem=send_sems.at[mir_sites + t], recv_sem=recv_sems.at[mir_sites + core],
                device_id=mirror[t], device_id_type=MESH,
            )
        )

        @pl.when(jnp.logical_not(mine[t]))
        def _():
            mir_copies[t].start()

        @pl.when(mine[t])
        def _():
            mir_recv[t] = mir_send[t]

    for t in range(2):

        @pl.when(jnp.logical_not(mine[t]))
        def _():
            pltpu.make_async_remote_copy(
                src_ref=mir_send.at[t], dst_ref=mir_recv.at[t],
                send_sem=send_sems.at[mir_sites + t], recv_sem=recv_sems.at[mir_sites + t],
                device_id=mirror[t], device_id_type=MESH,
            ).wait_recv()

    sym_halves = [
        0.5 * (current[:, t * ROWS : (t + 1) * ROWS] + mir_recv[t]) for t in range(2)
    ]
    for t in range(2):
        sym_out[:, t * ROWS : (t + 1) * ROWS] = sym_halves[t]
        sym_all[y, core, zl, t * ROWS : (t + 1) * ROWS] = sym_halves[t].T.astype(BF16)

    own_block = sym_all.at[y, core, zl]
    pair_block = sym_all.at[y, core, 1 - zl]
    pair_copy = send(own_block, own_block, z_pair)
    up_own = send(own_block, own_block, y_up)
    down_own = send(own_block, own_block, y_down)
    pair_copy.wait_recv()
    up_pair = send(pair_block, pair_block, y_up)
    down_pair = send(pair_block, pair_block, y_down)
    blocks = sym_all.at[y, core]
    sib_copies = [(y, send(blocks, blocks, sibling))]
    up_own.wait_recv()
    up_pair.wait_recv()
    below = sym_all.at[turn(y, -1, NY), core]
    up = send(below, below, y_up)
    sib_copies.append((turn(y, -1, NY), send(below, below, sibling)))
    down_own.wait_recv()
    down_pair.wait_recv()
    above = sym_all.at[turn(y, 1, NY), core]
    down = send(above, above, y_down)
    sib_copies.append((turn(y, 1, NY), send(above, above, sibling)))
    for d in (0, -1, 1, 2):
        fit_b[3](d)
        fit_a[3](d)
    up.wait_recv()
    below = sym_all.at[turn(y, -2, NY), core]
    up = send(below, below, y_up)
    sib_copies.append((turn(y, -2, NY), send(below, below, sibling)))
    down.wait_recv()
    above = sym_all.at[turn(y, 2, NY), core]
    down = send(above, above, y_down)
    sib_copies.append((turn(y, 2, NY), send(above, above, sibling)))
    up.wait_recv()
    low = sym_all.at[turn(y, -3, NY), core, 0]
    far_up = send(low, low, y_up)
    below = sym_all.at[turn(y, -3, NY), core]
    sib_copies.append((turn(y, -3, NY), send(below, below, sibling)))
    down.wait_recv()
    high = sym_all.at[turn(y, 3, NY), core, 1]
    far_down = send(high, high, y_down)
    above = sym_all.at[turn(y, 3, NY), core]
    sib_copies.append((turn(y, 3, NY), send(above, above, sibling)))
    far_up.wait_recv()
    far_down.wait_recv()
    across = sym_all.at[turn(y, 4, NY), core]
    sib_copies.append((turn(y, 4, NY), send(across, across, sibling)))

    own_fit.wait()
    fit_b[4]()
    fit_a[4]()
    acc[...] = jnp.zeros(acc.shape, F32)
    for k, copy in sib_copies:
        copy.wait_recv()
        panel = jnp.concatenate(
            [sym_all[k, 0, 0], sym_all[k, 1, 0], sym_all[k, 0, 1], sym_all[k, 1, 1]], axis=1
        )
        right = jnp.concatenate([fit_all[k * 2], fit_all[k * 2 + 1]], axis=0)
        acc[...] += jnp.dot(panel, right, preferred_element_type=F32)
    gamma_out[...] = acc[...].astype(BF16)

    for copy in sent:
        copy.wait_send()
    for t in range(2):

        @pl.when(jnp.logical_not(mine[t]))
        def _():
            mir_copies[t].wait_send()


def lookup(values_table, indices):
    extent = values_table.shape[0]
    matches = indices[:, None] == jnp.arange(extent, dtype=jnp.int32)[None, :]
    return jnp.sum(jnp.where(matches, values_table[None, :], 0.0), axis=1)


def body(start_amps, exchange_ints, fitted_ints, pao_energy, occ_fock, domains, pair_list):
    row = lax.axis_index("row")
    col = lax.axis_index("col")
    first, second = row // 4, col // 2
    orbits = jnp.arange(NORB, dtype=jnp.int32)
    first_fock = lax.dynamic_index_in_dim(occ_fock, first, 0, keepdims=False)
    second_fock = lax.dynamic_index_in_dim(occ_fock, second, 0, keepdims=False)
    first_own = jnp.sum(jnp.where(orbits == first, first_fock, 0.0))
    second_own = jnp.sum(jnp.where(orbits == second, second_fock, 0.0))
    first_off = jnp.where(orbits == first, 0.0, first_fock)
    second_off = jnp.where(orbits == second, 0.0, second_fock)
    listed = jnp.any((pair_list[:, 0] == first) & (pair_list[:, 1] == second)).astype(F32)
    scal = jnp.concatenate([first_off, second_off, jnp.broadcast_to(listed, (NORB,))])
    first_dom = lax.dynamic_index_in_dim(domains, first, 0, keepdims=False)
    second_dom = lax.dynamic_index_in_dim(domains, second, 0, keepdims=False)
    own_row_dom = first_dom.reshape(2, 2, ROWS).transpose(1, 0, 2).reshape(DOM, 1)
    own_col_dom = second_dom.reshape(1, DOM)
    row_paos = lax.dynamic_slice_in_dim(first_dom, lax.rem(row, 4) * ROWS, ROWS)
    col_paos = lax.dynamic_slice_in_dim(second_dom, lax.rem(col, 2) * COLS, COLS)
    row_level = (lookup(pao_energy, row_paos) - first_own)[:, None]
    col_level = (lookup(pao_energy, col_paos) - second_own)[None, :]
    vmem = pl.BlockSpec(memory_space=pltpu.VMEM)
    smem = pl.BlockSpec(memory_space=pltpu.SMEM)
    hbm = pl.BlockSpec(memory_space=pl.ANY)
    width = fitted_ints.shape[1]
    return pl.pallas_call(
        kernel,
        out_shape=(
            jax.ShapeDtypeStruct((ROWS, COLS), F32),
            jax.ShapeDtypeStruct((COLS, width), BF16),
        ),
        in_specs=[vmem, vmem, hbm, smem, vmem, vmem, vmem, vmem, vmem, vmem],
        out_specs=(vmem, vmem),
        scratch_shapes=[
            pltpu.VMEM((NX * NZ, COLS, width), BF16),
            pltpu.VMEM((ITERS, NORB, ROWS, COLS), BF16),
            pltpu.VMEM((ITERS, NORB, ROWS, COLS), BF16),
            pltpu.VMEM((ITERS, 2, 2, ROWS, COLS), F32),
            pltpu.VMEM((ITERS, 2, ROWS, COLS), F32),
            pltpu.VMEM((ITERS, ROWS, COLS), F32),
            pltpu.VMEM((ITERS, ROWS, COLS), F32),
            pltpu.VMEM((ITERS, 2, ROWS, COLS), F32),
            pltpu.VMEM((ITERS, ROWS, COLS), F32),
            pltpu.VMEM((NORB, DOM, ROWS), BF16),
            pltpu.VMEM((NORB, COLS, DOM), BF16),
            pltpu.VMEM((2, ROWS, ROWS), F32),
            pltpu.VMEM((2, ROWS, ROWS), F32),
            pltpu.VMEM((NY, 2, 2, COLS, ROWS), BF16),
            pltpu.VMEM((COLS, width), F32),
            pltpu.SemaphoreType.DMA((MAX_COPIES,)),
            pltpu.SemaphoreType.DMA((MAX_COPIES,)),
            pltpu.SemaphoreType.DMA,
        ],
        compiler_params=pltpu.CompilerParams(
            collective_id=0, has_side_effects=True, vmem_limit_bytes=48 * 1024 * 1024
        ),
        cost_estimate=pl.CostEstimate(flops=2_000_000_000, bytes_accessed=20_000_000, transcendentals=0),
    )(
        start_amps, exchange_ints, fitted_ints, scal, domains, domains.T, own_row_dom, own_col_dom,
        row_level, col_level,
    )


def solution(mesh):
    return jax.shard_map(
        body,
        mesh=mesh,
        in_specs=(P("row", "col"), P("row", "col"), P("col", "row"), P(), P(), P(), P()),
        out_specs=(P("row", "col"), P("col", "row")),
        check_vma=False,
    )
```

```python
import jax
import jax.numpy as jnp
from jax import lax
from jax.experimental import pallas as pl
from jax.experimental.pallas import tpu as pltpu
from jax.sharding import PartitionSpec as P

ITERS = 2
MESH = pl.DeviceIdType.MESH
F32 = jnp.float32
BF16 = jnp.bfloat16
ROWS, COLS, DOM, NORB = 128, 256, 512, 8
NY, NX, NZ = 8, 4, 4
FIRST_ROWS = 192
MAX_COPIES = 128


def turn(place, by, count):
    return lax.rem(place + (by + count), count)


def kernel(
    amps, exch, fitted, energy, fock, dom, pairs,
    sym_out, gamma_out,
    fit_all, left_all, right_all, left_part, left_sib, right_part, right_recv,
    left_hot, right_hot, levels, mir_send, mir_recv, sym_all, acc, send_sems, recv_sems, own_sem,
):
    row = lax.axis_index("row")
    col = lax.axis_index("col")
    y, quarter = row // 4, lax.rem(row, 4)
    zl, core = quarter // 2, lax.rem(quarter, 2)
    x, zh = col // 4, lax.rem(col, 4)
    b2, half = zh // 2, lax.rem(zh, 2)
    orb = col // 2

    def device(y_=y, zl_=zl, core_=core, x_=x, zh_=zh):
        return {"row": y_ * 4 + zl_ * 2 + core_, "col": x_ * 4 + zh_}

    y_up, y_down = device(y_=turn(y, 1, NY)), device(y_=turn(y, -1, NY))
    x_far = device(x_=turn(x, 2, NX))
    x_up, x_down = device(x_=turn(x, 1, NX)), device(x_=turn(x, -1, NX))
    z_up, z_down = device(zh_=turn(zh, 1, NZ)), device(zh_=turn(zh, -1, NZ))
    z_far = device(zh_=turn(zh, 2, NZ))
    z_pair = device(zl_=1 - zl)
    sibling = device(core_=1 - core)
    half_pair = device(zh_=b2 * 2 + 1 - half)
    diagonal = row // 2 == col
    mirror = [
        {"row": col * 2 + t, "col": row // 2} for t in range(2)
    ]
    mine = [jnp.logical_and(diagonal, core == t) for t in range(2)]

    barrier = pltpu.get_barrier_semaphore()
    partners = [y_up, y_down, x_up, x_down, x_far, z_up, z_down, z_far, z_pair, sibling]
    for partner in partners:
        pl.semaphore_signal(barrier, inc=1, device_id=partner, device_id_type=MESH)
    for t in range(2):

        @pl.when(jnp.logical_not(mine[t]))
        def _():
            pl.semaphore_signal(barrier, inc=1, device_id=mirror[t], device_id_type=MESH)

    pl.semaphore_wait(barrier, len(partners) + 2 - diagonal.astype(jnp.int32))

    sent = []
    sites = [0]

    def send(src, dst, target):
        site = sites[0]
        sites[0] += 1
        copy = pltpu.make_async_remote_copy(
            src_ref=src, dst_ref=dst, send_sem=send_sems.at[site], recv_sem=recv_sems.at[site],
            device_id=target, device_id_type=MESH,
        )
        copy.start()
        sent.append(copy)
        return copy

    def fit_gather(low, count, first_is_z):
        if first_is_z:
            one, two, n = zh, x, NZ
            one_up, one_down, two_up, two_down = z_up, z_down, x_up, x_down
            slot = lambda i, j: j * 4 + i
        else:
            one, two, n = x, zh, NX
            one_up, one_down, two_up, two_down = x_up, x_down, z_up, z_down
            slot = lambda i, j: i * 4 + j

        def at(i, j, piece=None):
            if piece is None:
                return fit_all.at[slot(i, j), pl.ds(low, count), :]
            return fit_all.at[slot(i, j), pl.ds(low + piece * (count // 2), count // 2), :]

        offsets = (0, -1, 1, 2)
        held = {}
        state = {}

        def along_two(d, src=None):
            i = turn(one, d, n)
            src = at(i, two) if src is None else src
            held[d] = (send(src, at(i, two), two_up), send(src, at(i, two), two_down))

        def start():
            own = fitted.at[pl.ds(low, count), :]
            state["up"] = send(own, at(one, two), one_up)
            state["down"] = send(own, at(one, two), one_down)
            along_two(0, own)

        def step_one():
            state["up"].wait_recv()
            i = turn(one, -1, n)
            state["far_up"] = send(at(i, two, 0), at(i, two, 0), one_up)
            along_two(-1)
            state["down"].wait_recv()
            i = turn(one, 1, n)
            state["far_down"] = send(at(i, two, 1), at(i, two, 1), one_down)
            along_two(1)

        def step_two():
            state["far_up"].wait_recv()
            state["far_down"].wait_recv()
            along_two(2)

        far = {}

        def step_three(d):
            up, down = held[d]
            i = turn(one, d, n)
            up.wait_recv()
            j = turn(two, -1, n)
            first = send(at(i, j, 0), at(i, j, 0), two_up)
            down.wait_recv()
            j = turn(two, 1, n)
            far[d] = (first, send(at(i, j, 1), at(i, j, 1), two_down))

        def step_four():
            for d in offsets:
                for copy in far[d]:
                    copy.wait_recv()

        return start, step_one, step_two, step_three, step_four

    fit_a = fit_gather(0, FIRST_ROWS, True)
    fit_b = fit_gather(FIRST_ROWS, COLS - FIRST_ROWS, False)
    own_fit = pltpu.make_async_copy(fitted, fit_all.at[col], own_sem)

    def listed():
        found = jnp.zeros((), jnp.bool_)
        for p in range(pairs.shape[1]):
            found = found | ((pairs[0, p] == y) & (pairs[1, p] == orb))
        return jnp.where(found, 1.0, 0.0)

    def off_diagonal(own, k):
        return jnp.where(own == k, 0.0, fock[own, k])

    def prepare():
        domains = dom[...].astype(F32)
        columns = jnp.concatenate([domains, jnp.zeros((ROWS - NORB, DOM), F32)], axis=0).T
        lanes = lax.broadcasted_iota(jnp.int32, (DOM, ROWS), 1)

        def column_of(k):
            return jnp.sum(jnp.where(lanes == k, columns, 0.0), axis=1, keepdims=True)

        levels[2] = column_of(y)
        levels[3] = column_of(orb)
        own_rows = levels[2, pl.ds(pl.multiple_of(zl * 2 * ROWS, 2 * ROWS), 2 * ROWS), :]
        own_cols = dom[pl.ds(orb, 1), :].astype(F32)
        for k in range(NORB):
            picked = [
                dom[k : k + 1, pl.ds(pl.multiple_of((p * 2 + core) * ROWS, ROWS), ROWS)] for p in range(2)
            ]
            picked = jnp.concatenate(picked, axis=1).astype(F32)
            left_hot[k] = jnp.where(own_rows == picked, 1.0, 0.0).astype(BF16)
            levels[4] = columns[:, k : k + 1]
            picked = levels[4, pl.ds(pl.multiple_of(half * COLS, COLS), COLS), :]
            right_hot[k] = jnp.where(picked == own_cols, 1.0, 0.0).astype(BF16)

        def level_of(paos):
            found = jnp.zeros((paos.shape[0], ROWS), F32)
            lane = lax.broadcasted_iota(jnp.int32, found.shape, 1).astype(F32)
            for r in range(energy.shape[0]):
                found += jnp.where(paos == lane + r * ROWS, energy[r : r + 1, :], 0.0)
            return jnp.sum(found, axis=1, keepdims=True)

        row_paos = levels[2, pl.ds(pl.multiple_of(quarter * ROWS, ROWS), ROWS), :]
        col_paos = levels[3, pl.ds(pl.multiple_of(half * COLS, COLS), COLS), :]
        row_level = level_of(row_paos) - fock[y, y]
        col_level = level_of(col_paos) - fock[orb, orb]
        return jnp.broadcast_to(row_level, (ROWS, COLS)) + jnp.broadcast_to(col_level, (COLS, ROWS)).T

    def panel_gather(at, between, arrived):
        ends = [lambda: None] * 8 if between is None else between
        pair = send(at(y, zl), at(y, zl), z_pair)
        ups = [send(at(y, zl), at(y, zl), y_up)]
        downs = [send(at(y, zl), at(y, zl), y_down)]
        ends[0]()
        pair.wait_recv()
        ups.append(send(at(y, 1 - zl), at(y, 1 - zl), y_up))
        downs.append(send(at(y, 1 - zl), at(y, 1 - zl), y_down))
        arrived(y, None)
        for distance in (1, 2, 3):
            below, above = turn(y, -distance, NY), turn(y, distance, NY)
            for p, place in enumerate((zl, 1 - zl)):
                ups[p].wait_recv()
                if distance < 3 or p == 0:
                    ups[p] = send(at(below, place), at(below, place), y_up)
                downs[p].wait_recv()
                if distance < 3 or p == 1:
                    downs[p] = send(at(above, place), at(above, place), y_down)
                ends[distance * 2 - 1 + p]()
            arrived(below, distance)
            arrived(above, distance)
        ups[0].wait_recv()
        downs[1].wait_recv()
        arrived(turn(y, 4, NY), 4)
        ends[7]()

    def iteration(t, current, first):
        rounded = current.astype(BF16)
        left_all[t, y, zl] = rounded
        right_all[t, orb] = rounded
        lefts, rights = left_all.at[t], right_all.at[t]
        other = x * 2 + 1 - b2
        far = send(rights.at[orb], rights.at[orb], z_far)
        x_one = [send(rights.at[orb], rights.at[orb], to) for to in (x_up, x_down, x_far)]
        x_two = []
        left_part[t] = jnp.zeros((2, ROWS, COLS), F32)
        right_part[t] = jnp.zeros((2, ROWS, COLS), F32)

        def left_add(k, distance):
            if distance is not None:
                block = left_all[t, k].reshape(2 * ROWS, COLS)
                term = jnp.dot(left_hot[k], block, preferred_element_type=F32) * off_diagonal(y, k)
                left_part[t] += term.reshape(2, ROWS, COLS)

        def right_add(k):
            term = jnp.dot(right_all[t, k], right_hot[k], preferred_element_type=F32)
            term = term * off_diagonal(orb, k)
            right_part[t, 0] += term[:, :COLS]
            right_part[t, 1] += term[:, COLS:]

        def right_far():
            far.wait_recv()
            x_two.extend(send(rights.at[other], rights.at[other], to) for to in (x_up, x_down, x_far))

        def right_one():
            right_add(other)
            for copy, by in zip(x_one, (-1, 1, 2)):
                copy.wait_recv()
                right_add(turn(x, by, NX) * 2 + b2)

        right_copy = []

        def right_two():
            for copy, by in zip(x_two, (-1, 1, 2)):
                copy.wait_recv()
                right_add(turn(x, by, NX) * 2 + 1 - b2)
            right_copy.append(send(right_part.at[t, 1 - half], right_recv.at[t], half_pair))

        def nothing():
            pass

        panel_gather(
            lambda k, p: lefts.at[k, p],
            (first, nothing, right_far, nothing, right_one, nothing, right_two, nothing),
            left_add,
        )
        sib_copy = send(left_part.at[t, 1 - core], left_sib.at[t], sibling)
        right_copy[0].wait_recv()
        right_term = right_part[t, half] + right_recv[t]
        sib_copy.wait_recv()
        left_term = left_part[t, core] + left_sib[t]
        return weight * ((left_term + right_term - exch[...].astype(F32)) / acc[:ROWS, :COLS])

    def start_fitted():
        fit_a[0]()
        fit_b[0]()
        own_fit.start()
        acc[:ROWS, :COLS] = prepare()

    def fit_one():
        fit_b[1]()
        fit_a[1]()

    def fit_two():
        fit_b[2]()
        fit_a[2]()

    weight = listed()
    current = iteration(0, amps[...], start_fitted)
    fit_one()
    current = iteration(1, current, lambda: None)
    fit_two()

    mir_sites = sites[0]
    sites[0] += 2
    mir_copies = []
    for t in range(2):
        mir_send[t] = current[:, t * ROWS : (t + 1) * ROWS].T
        mir_copies.append(
            pltpu.make_async_remote_copy(
                src_ref=mir_send.at[t], dst_ref=mir_recv.at[core],
                send_sem=send_sems.at[mir_sites + t], recv_sem=recv_sems.at[mir_sites + core],
                device_id=mirror[t], device_id_type=MESH,
            )
        )

        @pl.when(jnp.logical_not(mine[t]))
        def _():
            mir_copies[t].start()

        @pl.when(mine[t])
        def _():
            mir_recv[t] = mir_send[t]

    for t in range(2):

        @pl.when(jnp.logical_not(mine[t]))
        def _():
            pltpu.make_async_remote_copy(
                src_ref=mir_send.at[t], dst_ref=mir_recv.at[t],
                send_sem=send_sems.at[mir_sites + t], recv_sem=recv_sems.at[mir_sites + t],
                device_id=mirror[t], device_id_type=MESH,
            ).wait_recv()

    sym_halves = [
        0.5 * (current[:, t * ROWS : (t + 1) * ROWS] + mir_recv[t]) for t in range(2)
    ]
    for t in range(2):
        sym_out[:, t * ROWS : (t + 1) * ROWS] = sym_halves[t]
        sym_all[y, core, zl, t * ROWS : (t + 1) * ROWS] = sym_halves[t].T.astype(BF16)

    sib_copies = []

    def forward(k, distance):
        blocks = sym_all.at[k, core]
        sib_copies.append((k, send(blocks, blocks, sibling)))

    def fit_three(*offsets):
        def run():
            for d in offsets:
                fit_b[3](d)
                fit_a[3](d)

        return run

    def nothing():
        pass

    panel_gather(
        lambda k, p: sym_all.at[k, core, p],
        (nothing, nothing, fit_three(0), nothing, fit_three(-1), nothing, fit_three(1), fit_three(2)),
        forward,
    )
    own_fit.wait()
    fit_b[4]()
    fit_a[4]()
    acc[...] = jnp.zeros(acc.shape, F32)
    for k, copy in sib_copies:
        copy.wait_recv()
        panel = jnp.concatenate(
            [sym_all[k, 0, 0], sym_all[k, 1, 0], sym_all[k, 0, 1], sym_all[k, 1, 1]], axis=1
        )
        right = jnp.concatenate([fit_all[k * 2], fit_all[k * 2 + 1]], axis=0)
        acc[...] += jnp.dot(panel, right, preferred_element_type=F32)
    gamma_out[...] = acc[...].astype(BF16)

    for copy in sent:
        copy.wait_send()
    for t in range(2):

        @pl.when(jnp.logical_not(mine[t]))
        def _():
            mir_copies[t].wait_send()


def body(start_amps, exchange_ints, fitted_ints, pao_energy, occ_fock, domains, pair_list):
    vmem = pl.BlockSpec(memory_space=pltpu.VMEM)
    smem = pl.BlockSpec(memory_space=pltpu.SMEM)
    hbm = pl.BlockSpec(memory_space=pl.ANY)
    width = fitted_ints.shape[1]
    return pl.pallas_call(
        kernel,
        out_shape=(
            jax.ShapeDtypeStruct((ROWS, COLS), F32),
            jax.ShapeDtypeStruct((COLS, width), BF16),
        ),
        in_specs=[vmem, vmem, hbm, vmem, smem, vmem, smem],
        out_specs=(vmem, vmem),
        scratch_shapes=[
            pltpu.VMEM((NX * NZ, COLS, width), BF16),
            pltpu.VMEM((ITERS, NORB, 2, ROWS, COLS), BF16),
            pltpu.VMEM((ITERS, NORB, ROWS, COLS), BF16),
            pltpu.VMEM((ITERS, 2, ROWS, COLS), F32),
            pltpu.VMEM((ITERS, ROWS, COLS), F32),
            pltpu.VMEM((ITERS, 2, ROWS, COLS), F32),
            pltpu.VMEM((ITERS, ROWS, COLS), F32),
            pltpu.VMEM((NORB, 2 * ROWS, 2 * ROWS), BF16),
            pltpu.VMEM((NORB, COLS, DOM), BF16),
            pltpu.VMEM((5, DOM, 1), F32),
            pltpu.VMEM((2, ROWS, ROWS), F32),
            pltpu.VMEM((2, ROWS, ROWS), F32),
            pltpu.VMEM((NY, 2, 2, COLS, ROWS), BF16),
            pltpu.VMEM((COLS, width), F32),
            pltpu.SemaphoreType.DMA((MAX_COPIES,)),
            pltpu.SemaphoreType.DMA((MAX_COPIES,)),
            pltpu.SemaphoreType.DMA,
        ],
        compiler_params=pltpu.CompilerParams(
            collective_id=0, has_side_effects=True, vmem_limit_bytes=48 * 1024 * 1024
        ),
        cost_estimate=pl.CostEstimate(flops=2_000_000_000, bytes_accessed=20_000_000, transcendentals=0),
    )(
        start_amps, exchange_ints, fitted_ints, pao_energy.reshape(-1, ROWS), occ_fock, domains, pair_list.T
    )


def solution(mesh):
    return jax.shard_map(
        body,
        mesh=mesh,
        in_specs=(P("row", "col"), P("row", "col"), P("col", "row"), P(), P(), P(), P()),
        out_specs=(P("row", "col"), P("col", "row")),
        check_vma=False,
    )
```

```python
import jax
import jax.numpy as jnp
from jax import lax
from jax.experimental import pallas as pl
from jax.experimental.pallas import tpu as pltpu
from jax.sharding import PartitionSpec as P

ITERS = 2
MESH = pl.DeviceIdType.MESH
F32 = jnp.float32
BF16 = jnp.bfloat16
ROWS, COLS, DOM, NORB = 128, 256, 512, 8
NY, NX, NZ = 8, 4, 4
PIECES = ((0, 256, True),)
PLAN = {'start': [0], (0, 6): [1, 2], (0, 8): [4], (1, 2): [3], (1, 4): [5], (1, 8): [6], (2, 0): [7], (3, 4): [8, 9, 10, 11]}
MAX_COPIES = 256


def turn(place, by, count):
    return lax.rem(place + (by + count), count)


def kernel(
    amps_hbm, exch_hbm, fitted, energy_hbm, fock, dom_hbm, pairs,
    sym_out, gamma_out,
    fit_all, left_all, right_all, left_part, left_sib, right_part, right_recv,
    left_hot, right_hot, levels, mir_send, mir_recv, sym_all, acc, amps, exch, energy, dom,
    send_sems, recv_sems, own_sem, load_sems,
):
    row = lax.axis_index("row")
    col = lax.axis_index("col")
    y, quarter = row // 4, lax.rem(row, 4)
    zl, core = quarter // 2, lax.rem(quarter, 2)
    x, zh = col // 4, lax.rem(col, 4)
    b2, half = zh // 2, lax.rem(zh, 2)
    orb = col // 2

    def device(y_=y, zl_=zl, core_=core, x_=x, zh_=zh):
        return {"row": y_ * 4 + zl_ * 2 + core_, "col": x_ * 4 + zh_}

    y_up, y_down = device(y_=turn(y, 1, NY)), device(y_=turn(y, -1, NY))
    x_far = device(x_=turn(x, 2, NX))
    x_up, x_down = device(x_=turn(x, 1, NX)), device(x_=turn(x, -1, NX))
    z_up, z_down = device(zh_=turn(zh, 1, NZ)), device(zh_=turn(zh, -1, NZ))
    z_far = device(zh_=turn(zh, 2, NZ))
    z_pair = device(zl_=1 - zl)
    sibling = device(core_=1 - core)
    half_pair = device(zh_=b2 * 2 + 1 - half)
    diagonal = row // 2 == col
    mirror = [
        {"row": col * 2 + t, "col": row // 2} for t in range(2)
    ]
    mine = [jnp.logical_and(diagonal, core == t) for t in range(2)]

    loads = [
        pltpu.make_async_copy(src, dst, load_sems.at[n])
        for n, (src, dst) in enumerate(
            ((amps_hbm, amps), (dom_hbm, dom), (energy_hbm, energy), (exch_hbm, exch))
        )
    ]
    for load in loads:
        load.start()
    barrier = pltpu.get_barrier_semaphore()
    partners = [y_up, y_down, x_up, x_down, x_far, z_up, z_down, z_far, z_pair, sibling]
    for partner in partners:
        pl.semaphore_signal(barrier, inc=1, device_id=partner, device_id_type=MESH)
    for t in range(2):

        @pl.when(jnp.logical_not(mine[t]))
        def _():
            pl.semaphore_signal(barrier, inc=1, device_id=mirror[t], device_id_type=MESH)

    pl.semaphore_wait(barrier, len(partners) + 2 - diagonal.astype(jnp.int32))

    sent = []
    sites = [0]

    def send(src, dst, target):
        site = sites[0]
        sites[0] += 1
        copy = pltpu.make_async_remote_copy(
            src_ref=src, dst_ref=dst, send_sem=send_sems.at[site], recv_sem=recv_sems.at[site],
            device_id=target, device_id_type=MESH,
        )
        copy.start()
        sent.append(copy)
        return copy

    def fit_gather(low, count, first_is_z):
        if first_is_z:
            one, two, n = zh, x, NZ
            one_up, one_down, two_up, two_down = z_up, z_down, x_up, x_down
            slot = lambda i, j: j * 4 + i
        else:
            one, two, n = x, zh, NX
            one_up, one_down, two_up, two_down = x_up, x_down, z_up, z_down
            slot = lambda i, j: i * 4 + j

        def at(i, j, piece=None):
            if piece is None:
                return fit_all.at[slot(i, j), pl.ds(low, count), :]
            return fit_all.at[slot(i, j), pl.ds(low + piece * (count // 2), count // 2), :]

        held = {}
        state = {}
        far = {}

        def along_two(d, src=None):
            i = turn(one, d, n)
            src = at(i, two) if src is None else src
            held[d] = (send(src, at(i, two), two_up), send(src, at(i, two), two_down))

        def start():
            own = fitted.at[pl.ds(low, count), :]
            state["up"] = send(own, at(one, two), one_up)
            state["down"] = send(own, at(one, two), one_down)
            along_two(0, own)

        def from_below():
            state["up"].wait_recv()
            i = turn(one, -1, n)
            state["far_up"] = send(at(i, two, 0), at(i, two, 0), one_up)
            along_two(-1)

        def from_above():
            state["down"].wait_recv()
            i = turn(one, 1, n)
            state["far_down"] = send(at(i, two, 1), at(i, two, 1), one_down)
            along_two(1)

        def from_far():
            state["far_up"].wait_recv()
            state["far_down"].wait_recv()
            along_two(2)

        def across(d):
            def run():
                up, down = held[d]
                i = turn(one, d, n)
                up.wait_recv()
                j = turn(two, -1, n)
                first = send(at(i, j, 0), at(i, j, 0), two_up)
                down.wait_recv()
                j = turn(two, 1, n)
                far[d] = (first, send(at(i, j, 1), at(i, j, 1), two_down))

            return run

        def last(d):
            def run():
                for copy in far[d]:
                    copy.wait_recv()

            return run

        return [start, from_below, from_above, from_far] + [across(d) for d in (0, -1, 1, 2)] + [
            last(d) for d in (0, -1, 1, 2)
        ]

    pieces = [fit_gather(*piece) for piece in PIECES]
    fit_done = set()

    def fit_stage(stages):
        for stage in stages:
            for number, piece in enumerate(pieces):
                if (stage, number) not in fit_done:
                    fit_done.add((stage, number))
                    piece[stage]()

    def hook(name):
        return lambda: fit_stage(PLAN.get(name, ()))

    own_fit = pltpu.make_async_copy(fitted, fit_all.at[col], own_sem)

    def listed():
        found = jnp.zeros((), jnp.bool_)
        for p in range(pairs.shape[1]):
            found = found | ((pairs[0, p] == y) & (pairs[1, p] == orb))
        return jnp.where(found, 1.0, 0.0)

    def off_diagonal(own, k):
        return jnp.where(own == k, 0.0, fock[own, k])

    def prepare():
        for load in loads[1:]:
            load.wait()
        domains = dom[...].astype(F32)
        columns = jnp.concatenate([domains, jnp.zeros((ROWS - NORB, DOM), F32)], axis=0).T
        lanes = lax.broadcasted_iota(jnp.int32, (DOM, ROWS), 1)

        def column_of(k):
            return jnp.sum(jnp.where(lanes == k, columns, 0.0), axis=1, keepdims=True)

        levels[2] = column_of(y)
        levels[3] = column_of(orb)
        own_rows = levels[2, pl.ds(pl.multiple_of(zl * 2 * ROWS, 2 * ROWS), 2 * ROWS), :]
        own_cols = dom[pl.ds(orb, 1), :].astype(F32)
        for k in range(NORB):
            picked = [
                dom[k : k + 1, pl.ds(pl.multiple_of((p * 2 + core) * ROWS, ROWS), ROWS)] for p in range(2)
            ]
            picked = jnp.concatenate(picked, axis=1).astype(F32)
            left_hot[k] = jnp.where(own_rows == picked, 1.0, 0.0).astype(BF16)
            levels[4] = columns[:, k : k + 1]
            picked = levels[4, pl.ds(pl.multiple_of(half * COLS, COLS), COLS), :]
            right_hot[k] = jnp.where(picked == own_cols, 1.0, 0.0).astype(BF16)

        def level_of(paos):
            found = jnp.zeros((paos.shape[0], ROWS), F32)
            lane = lax.broadcasted_iota(jnp.int32, found.shape, 1).astype(F32)
            for r in range(energy.shape[0]):
                found += jnp.where(paos == lane + r * ROWS, energy[r : r + 1, :], 0.0)
            return jnp.sum(found, axis=1, keepdims=True)

        row_paos = levels[2, pl.ds(pl.multiple_of(quarter * ROWS, ROWS), ROWS), :]
        col_paos = levels[3, pl.ds(pl.multiple_of(half * COLS, COLS), COLS), :]
        row_level = level_of(row_paos) - fock[y, y]
        col_level = level_of(col_paos) - fock[orb, orb]
        return jnp.broadcast_to(row_level, (ROWS, COLS)) + jnp.broadcast_to(col_level, (COLS, ROWS)).T

    def panel_gather(at, between, arrived):
        parts = range(2)
        streams = [(zl, i) for i in parts] + [(1 - zl, i) for i in parts]
        pairs_in = [send(at(y, *at_), at(y, *at_), z_pair) for at_ in streams[:2]]
        ups = [send(at(y, *at_), at(y, *at_), y_up) for at_ in streams[:2]]
        downs = [send(at(y, *at_), at(y, *at_), y_down) for at_ in streams[:2]]
        between[0]()
        for copy, at_ in zip(pairs_in, streams[2:]):
            copy.wait_recv()
            ups.append(send(at(y, *at_), at(y, *at_), y_up))
            downs.append(send(at(y, *at_), at(y, *at_), y_down))
        arrived(y, None)
        for distance in (1, 2, 3):
            below, above = turn(y, -distance, NY), turn(y, distance, NY)
            for n, at_ in enumerate(streams):
                ups[n].wait_recv()
                if distance < 3 or n < 2:
                    ups[n] = send(at(below, *at_), at(below, *at_), y_up)
                downs[n].wait_recv()
                if distance < 3 or n >= 2:
                    downs[n] = send(at(above, *at_), at(above, *at_), y_down)
                if n % 2 == 1:
                    between[distance * 2 - 1 + n // 2]()
            arrived(below, distance)
            arrived(above, distance)
        for n in range(4):
            (ups if n < 2 else downs)[n].wait_recv()
        arrived(turn(y, 4, NY), 4)
        between[7]()

    def two(f, g):
        def run():
            f()
            g()

        return run

    def iteration(t, current, first):
        rounded = current.astype(BF16)
        left_all[t, y, zl] = rounded
        right_all[t, orb] = rounded
        lefts, rights = left_all.at[t], right_all.at[t]
        other = x * 2 + 1 - b2
        far = send(rights.at[orb], rights.at[orb], z_far)
        x_one = [send(rights.at[orb], rights.at[orb], to) for to in (x_up, x_down, x_far)]
        x_two = []
        left_part[t] = jnp.zeros((2, ROWS, COLS), F32)
        right_part[t] = jnp.zeros((2, ROWS, COLS), F32)

        def left_add(k, distance):
            if distance is not None:
                block = left_all[t, k].reshape(2 * ROWS, COLS)
                term = jnp.dot(left_hot[k], block, preferred_element_type=F32) * off_diagonal(y, k)
                left_part[t] += term.reshape(2, ROWS, COLS)

        def right_add(k):
            term = jnp.dot(right_all[t, k], right_hot[k], preferred_element_type=F32)
            term = term * off_diagonal(orb, k)
            right_part[t, 0] += term[:, :COLS]
            right_part[t, 1] += term[:, COLS:]

        def right_far():
            far.wait_recv()
            x_two.extend(send(rights.at[other], rights.at[other], to) for to in (x_up, x_down, x_far))

        def right_one():
            right_add(other)
            for copy, by in zip(x_one, (-1, 1, 2)):
                copy.wait_recv()
                right_add(turn(x, by, NX) * 2 + b2)

        right_copy = []

        def right_two():
            for copy, by in zip(x_two, (-1, 1, 2)):
                copy.wait_recv()
                right_add(turn(x, by, NX) * 2 + 1 - b2)
            right_copy.append(send(right_part.at[t, 1 - half], right_recv.at[t], half_pair))

        def nothing():
            pass

        panel_gather(
            lambda k, p, i: lefts.at[k, p, pl.ds(i * (ROWS // 2), ROWS // 2)],
            tuple(two(f, hook((t, i))) for i, f in enumerate((first, nothing, right_far, nothing, right_one, nothing, right_two, nothing))),
            left_add,
        )
        sib_copy = send(left_part.at[t, 1 - core], left_sib.at[t], sibling)
        hook((t, 8))()
        right_copy[0].wait_recv()
        right_term = right_part[t, half] + right_recv[t]
        sib_copy.wait_recv()
        left_term = left_part[t, core] + left_sib[t]
        return weight * ((left_term + right_term - exch[...].astype(F32)) / acc[:ROWS, :COLS])

    def start_fitted():
        fit_stage(PLAN['start'])
        own_fit.start()
        acc[:ROWS, :COLS] = prepare()

    weight = listed()
    loads[0].wait()
    current = iteration(0, amps[...], start_fitted)
    hook((0, 9))()
    current = iteration(1, current, lambda: None)

    mir_sites = sites[0]
    sites[0] += 2
    mir_copies = []
    for t in range(2):
        mir_send[t] = current[:, t * ROWS : (t + 1) * ROWS].T
        mir_copies.append(
            pltpu.make_async_remote_copy(
                src_ref=mir_send.at[t], dst_ref=mir_recv.at[core],
                send_sem=send_sems.at[mir_sites + t], recv_sem=recv_sems.at[mir_sites + core],
                device_id=mirror[t], device_id_type=MESH,
            )
        )

        @pl.when(jnp.logical_not(mine[t]))
        def _():
            mir_copies[t].start()

        @pl.when(mine[t])
        def _():
            mir_recv[t] = mir_send[t]

    hook((2, 0))()
    for t in range(2):

        @pl.when(jnp.logical_not(mine[t]))
        def _():
            pltpu.make_async_remote_copy(
                src_ref=mir_send.at[t], dst_ref=mir_recv.at[t],
                send_sem=send_sems.at[mir_sites + t], recv_sem=recv_sems.at[mir_sites + t],
                device_id=mirror[t], device_id_type=MESH,
            ).wait_recv()

    sym_halves = [
        0.5 * (current[:, t * ROWS : (t + 1) * ROWS] + mir_recv[t]) for t in range(2)
    ]
    for t in range(2):
        sym_out[:, t * ROWS : (t + 1) * ROWS] = sym_halves[t]
        sym_all[y, core, zl, t * ROWS : (t + 1) * ROWS] = sym_halves[t].T.astype(BF16)

    sib_copies = []

    def forward(k, distance):
        blocks = sym_all.at[k, core]
        sib_copies.append((k, send(blocks, blocks, sibling)))

    def nothing():
        pass

    panel_gather(
        lambda k, p, i: sym_all.at[k, core, p, pl.ds(i * ROWS, ROWS)],
        tuple(hook((3, i)) for i in range(8)),
        forward,
    )
    own_fit.wait()
    fit_stage(range(12))
    acc[...] = jnp.zeros(acc.shape, F32)
    for k, copy in sib_copies:
        copy.wait_recv()
        panel = jnp.concatenate(
            [sym_all[k, 0, 0], sym_all[k, 1, 0], sym_all[k, 0, 1], sym_all[k, 1, 1]], axis=1
        )
        right = jnp.concatenate([fit_all[k * 2], fit_all[k * 2 + 1]], axis=0)
        acc[...] += jnp.dot(panel, right, preferred_element_type=F32)
    gamma_out[...] = acc[...].astype(BF16)

    for copy in sent:
        copy.wait_send()
    for t in range(2):

        @pl.when(jnp.logical_not(mine[t]))
        def _():
            mir_copies[t].wait_send()


def body(start_amps, exchange_ints, fitted_ints, pao_energy, occ_fock, domains, pair_list):
    vmem = pl.BlockSpec(memory_space=pltpu.VMEM)
    smem = pl.BlockSpec(memory_space=pltpu.SMEM)
    hbm = pl.BlockSpec(memory_space=pl.ANY)
    width = fitted_ints.shape[1]
    return pl.pallas_call(
        kernel,
        out_shape=(
            jax.ShapeDtypeStruct((ROWS, COLS), F32),
            jax.ShapeDtypeStruct((COLS, width), BF16),
        ),
        in_specs=[hbm, hbm, hbm, hbm, smem, hbm, smem],
        out_specs=(vmem, vmem),
        scratch_shapes=[
            pltpu.VMEM((NX * NZ, COLS, width), BF16),
            pltpu.VMEM((ITERS, NORB, 2, ROWS, COLS), BF16),
            pltpu.VMEM((ITERS, NORB, ROWS, COLS), BF16),
            pltpu.VMEM((ITERS, 2, ROWS, COLS), F32),
            pltpu.VMEM((ITERS, ROWS, COLS), F32),
            pltpu.VMEM((ITERS, 2, ROWS, COLS), F32),
            pltpu.VMEM((ITERS, ROWS, COLS), F32),
            pltpu.VMEM((NORB, 2 * ROWS, 2 * ROWS), BF16),
            pltpu.VMEM((NORB, COLS, DOM), BF16),
            pltpu.VMEM((5, DOM, 1), F32),
            pltpu.VMEM((2, ROWS, ROWS), F32),
            pltpu.VMEM((2, ROWS, ROWS), F32),
            pltpu.VMEM((NY, 2, 2, COLS, ROWS), BF16),
            pltpu.VMEM((COLS, width), F32),
            pltpu.VMEM((ROWS, COLS), F32),
            pltpu.VMEM((ROWS, COLS), BF16),
            pltpu.VMEM((pao_energy.shape[0] // ROWS, ROWS), F32),
            pltpu.VMEM((NORB, DOM), jnp.int32),
            pltpu.SemaphoreType.DMA((MAX_COPIES,)),
            pltpu.SemaphoreType.DMA((MAX_COPIES,)),
            pltpu.SemaphoreType.DMA,
            pltpu.SemaphoreType.DMA((4,)),
        ],
        compiler_params=pltpu.CompilerParams(
            collective_id=0, has_side_effects=True, vmem_limit_bytes=60 * 1024 * 1024
        ),
        cost_estimate=pl.CostEstimate(flops=2_000_000_000, bytes_accessed=20_000_000, transcendentals=0),
    )(
        start_amps, exchange_ints, fitted_ints, pao_energy.reshape(-1, ROWS), occ_fock, domains, pair_list.T
    )


def solution(mesh):
    return jax.shard_map(
        body,
        mesh=mesh,
        in_specs=(P("row", "col"), P("row", "col"), P("col", "row"), P(), P(), P(), P()),
        out_specs=(P("row", "col"), P("col", "row")),
        check_vma=False,
    )
```

```python
import jax
import jax.numpy as jnp
from jax import lax
from jax.experimental import pallas as pl
from jax.experimental.pallas import tpu as pltpu
from jax.sharding import PartitionSpec as P

ITERS = 2
MESH = pl.DeviceIdType.MESH
F32 = jnp.float32
BF16 = jnp.bfloat16
ROWS, HALF, COLS, DOM, NORB = 128, 64, 256, 512, 8
NY, NX, NZ = 8, 4, 4
PIECE = 128
PLAN = {
    (0, 0): (('own', 0), ('x', 0, 0)),
    (0, 2): (('own', 1),),
    (0, 4): (('x', 0, 1),),
    (0, 7): (('near', 0), ('near', 1)),
    (0, 8): (('turn', 0, 0), ('turn', 0, 1)),
    (0, 9): (('x', -1, 0), ('x', -1, 1)),
    (1, 4): (('far', 0), ('far', 1)),
    (1, 6): (('turn', -1, 0), ('turn', -1, 1), ('x', 1, 0), ('x', 1, 1)),
    (2, 0): (('x', 2, 0), ('x', 2, 1), ('turn', 1, 0), ('turn', 1, 1)),
    (3, 4): (('turn', 2, 0), ('turn', 2, 1)),
}
MAX_COPIES = 256


def turn(place, by, count):
    return lax.rem(place + (by + count), count)


def kernel(
    amps_hbm, exch_hbm, fitted, energy_hbm, fock, dom_hbm, pairs,
    sym_out, gamma_out,
    fit_all, left_all, right_send, right_all, left_part, left_sib, right_part, right_recv,
    left_hot, right_hot, levels, mir_send, mir_recv, sym_all, acc, amps, exch, energy, dom,
    send_sems, recv_sems, own_sem, load_sems,
):
    row = lax.axis_index("row")
    col = lax.axis_index("col")
    y, quarter = row // 4, lax.rem(row, 4)
    zl, core = quarter // 2, lax.rem(quarter, 2)
    x, zh = col // 4, lax.rem(col, 4)
    b2, half = zh // 2, lax.rem(zh, 2)
    orb = col // 2

    def device(y_=y, zl_=zl, core_=core, x_=x, zh_=zh):
        return {"row": y_ * 4 + zl_ * 2 + core_, "col": x_ * 4 + zh_}

    y_up, y_down = device(y_=turn(y, 1, NY)), device(y_=turn(y, -1, NY))
    x_far = device(x_=turn(x, 2, NX))
    x_up, x_down = device(x_=turn(x, 1, NX)), device(x_=turn(x, -1, NX))
    z_up, z_down = device(zh_=turn(zh, 1, NZ)), device(zh_=turn(zh, -1, NZ))
    z_far = device(zh_=turn(zh, 2, NZ))
    z_other = device(zh_=(1 - b2) * 2 + 1 - half)
    z_pair = device(zl_=1 - zl)
    sibling = device(core_=1 - core)
    half_pair = device(zh_=b2 * 2 + 1 - half)
    diagonal = row // 2 == col
    mirror = [
        {"row": col * 2 + t, "col": row // 2} for t in range(2)
    ]
    mine = [jnp.logical_and(diagonal, core == t) for t in range(2)]

    loads = [
        pltpu.make_async_copy(src, dst, load_sems.at[n])
        for n, (src, dst) in enumerate(
            ((amps_hbm, amps), (dom_hbm, dom), (energy_hbm, energy), (exch_hbm, exch))
        )
    ]
    for load in loads:
        load.start()
    barrier = pltpu.get_barrier_semaphore()
    partners = [y_up, y_down, x_up, x_down, x_far, z_up, z_down, z_far, z_pair, sibling]
    for partner in partners:
        pl.semaphore_signal(barrier, inc=1, device_id=partner, device_id_type=MESH)
    for t in range(2):

        @pl.when(jnp.logical_not(mine[t]))
        def _():
            pl.semaphore_signal(barrier, inc=1, device_id=mirror[t], device_id_type=MESH)

    pl.semaphore_wait(barrier, len(partners) + 2 - diagonal.astype(jnp.int32))

    sent = []
    sites = [0]

    def send(src, dst, target):
        site = sites[0]
        sites[0] += 1
        copy = pltpu.make_async_remote_copy(
            src_ref=src, dst_ref=dst, send_sem=send_sems.at[site], recv_sem=recv_sems.at[site],
            device_id=target, device_id_type=MESH,
        )
        copy.start()
        sent.append(copy)
        return copy

    z_slot = {0: zh, -1: turn(zh, -1, NZ), 1: turn(zh, 1, NZ), 2: turn(zh, 2, NZ)}
    fit_sent = {}

    def fit_at(d, x_place, n, share=None):
        low, count = n * PIECE, PIECE
        if share is not None:
            low, count = low + share * (PIECE // 2), PIECE // 2
        return fit_all.at[x_place * NZ + z_slot[d], pl.ds(low, count), :]

    def fit_own_z(n):
        own = fitted.at[pl.ds(n * PIECE, PIECE), :]
        fit_sent["z", -1, n] = send(own, fit_at(0, x, n), z_up)
        fit_sent["z", 1, n] = send(own, fit_at(0, x, n), z_down)

    def fit_x(d, n):
        src = fitted.at[pl.ds(n * PIECE, PIECE), :] if d == 0 else fit_at(d, x, n)
        fit_sent["x", d, n] = [send(src, fit_at(d, x, n), to) for to in (x_up, x_down)]

    def fit_near_z(n):
        for d, share, to in ((-1, 0, z_up), (1, 1, z_down)):
            fit_sent["z", d, n].wait_recv()
            fit_sent["far", share, n] = send(fit_at(d, x, n, share), fit_at(d, x, n, share), to)

    def fit_far_z(n):
        for share in range(2):
            fit_sent["far", share, n].wait_recv()

    def fit_turn_x(d, n):
        up, down = fit_sent["x", d, n]
        last = []
        for copy, by, share, to in ((up, -1, 0, x_up), (down, 1, 1, x_down)):
            copy.wait_recv()
            block = fit_at(d, turn(x, by, NX), n, share)
            last.append(send(block, block, to))
        fit_sent["last", d, n] = last

    def fit_last(d, n):
        for copy in fit_sent["last", d, n]:
            copy.wait_recv()

    actions = {
        "own": fit_own_z, "near": fit_near_z, "far": fit_far_z, "x": fit_x, "turn": fit_turn_x,
        "last": fit_last,
    }

    def hook(*place):
        def run():
            for step in PLAN.get(place, ()):
                actions[step[0]](*step[1:])

        return run

    own_fit = pltpu.make_async_copy(fitted, fit_all.at[col], own_sem)

    def listed():
        found = jnp.zeros((), jnp.bool_)
        for p in range(pairs.shape[1]):
            found = found | ((pairs[0, p] == y) & (pairs[1, p] == orb))
        return jnp.where(found, 1.0, 0.0)

    def off_diagonal(own, k):
        return jnp.where(own == k, 0.0, fock[own, k])

    def prepare():
        for load in loads[1:]:
            load.wait()
        domains = dom[...].astype(F32)
        columns = jnp.concatenate([domains, jnp.zeros((ROWS - NORB, DOM), F32)], axis=0).T
        lanes = lax.broadcasted_iota(jnp.int32, (DOM, ROWS), 1)

        def column_of(k):
            return jnp.sum(jnp.where(lanes == k, columns, 0.0), axis=1, keepdims=True)

        levels[2] = column_of(y)
        levels[3] = column_of(orb)
        own_rows = levels[2, pl.ds(pl.multiple_of(zl * 2 * ROWS, 2 * ROWS), 2 * ROWS), :]
        own_cols = dom[pl.ds(orb, 1), :].astype(F32)
        for k in range(NORB):
            picked = [
                dom[k : k + 1, pl.ds(pl.multiple_of((p * 2 + core) * ROWS, ROWS), ROWS)] for p in range(2)
            ]
            picked = jnp.concatenate(picked, axis=1).astype(F32)
            left_hot[k] = jnp.where(own_rows == picked, 1.0, 0.0).astype(BF16)
            right_hot[k] = jnp.where(columns[:, k : k + 1] == own_cols, 1.0, 0.0).astype(BF16)

        def level_of(paos):
            found = jnp.zeros((paos.shape[0], ROWS), F32)
            lane = lax.broadcasted_iota(jnp.int32, found.shape, 1).astype(F32)
            for r in range(energy.shape[0]):
                found += jnp.where(paos == lane + r * ROWS, energy[r : r + 1, :], 0.0)
            return jnp.sum(found, axis=1, keepdims=True)

        row_paos = levels[2, pl.ds(pl.multiple_of(quarter * ROWS, ROWS), ROWS), :]
        col_paos = levels[3, pl.ds(pl.multiple_of(half * COLS, COLS), COLS), :]
        row_level = level_of(row_paos) - fock[y, y]
        col_level = level_of(col_paos) - fock[orb, orb]
        return jnp.broadcast_to(row_level, (ROWS, COLS)) + jnp.broadcast_to(col_level, (COLS, ROWS)).T

    def panel_gather(at, between, arrived):
        parts = range(2)
        streams = [(zl, i) for i in parts] + [(1 - zl, i) for i in parts]
        pairs_in = [send(at(y, *at_), at(y, *at_), z_pair) for at_ in streams[:2]]
        ups = [send(at(y, *at_), at(y, *at_), y_up) for at_ in streams[:2]]
        downs = [send(at(y, *at_), at(y, *at_), y_down) for at_ in streams[:2]]
        between[0]()
        for copy, at_ in zip(pairs_in, streams[2:]):
            copy.wait_recv()
            ups.append(send(at(y, *at_), at(y, *at_), y_up))
            downs.append(send(at(y, *at_), at(y, *at_), y_down))
        arrived(y, None)
        for distance in (1, 2, 3):
            below, above = turn(y, -distance, NY), turn(y, distance, NY)
            for n, at_ in enumerate(streams):
                ups[n].wait_recv()
                if distance < 3 or n < 2:
                    ups[n] = send(at(below, *at_), at(below, *at_), y_up)
                downs[n].wait_recv()
                if distance < 3 or n >= 2:
                    downs[n] = send(at(above, *at_), at(above, *at_), y_down)
                if n % 2 == 1:
                    between[distance * 2 - 1 + n // 2]()
            arrived(below, distance)
            arrived(above, distance)
        for n in range(4):
            (ups if n < 2 else downs)[n].wait_recv()
        arrived(turn(y, 4, NY), 4)
        between[7]()

    def two(f, g):
        def run():
            f()
            g()

        return run

    def iteration(t, current, first):
        rounded = current.astype(BF16)
        left_all[t, y, zl] = rounded
        right_send[t] = rounded.reshape(2, HALF, COLS)
        right_all[t, orb, half] = right_send[t, half]
        lefts, rights = left_all.at[t], right_all.at[t]
        other = x * 2 + 1 - b2
        sources = right_send.at[t]
        z_copies = [
            send(sources.at[1 - half], rights.at[orb, half], half_pair),
            send(sources.at[half], rights.at[orb, half], z_far),
            send(sources.at[1 - half], rights.at[orb, half], z_other),
        ]
        x_tos = (x_up, x_down, x_far)
        x_one = [send(rights.at[orb, half], rights.at[orb, half], to) for to in x_tos]
        x_two = []
        left_part[t] = jnp.zeros((2, ROWS, COLS), F32)
        right_part[t] = jnp.zeros((2, HALF, COLS), F32)

        def left_add(k, distance):
            if distance is not None:
                block = left_all[t, k].reshape(2 * ROWS, COLS)
                term = jnp.dot(left_hot[k], block, preferred_element_type=F32) * off_diagonal(y, k)
                left_part[t] += term.reshape(2, ROWS, COLS)

        def right_add(k):
            block = jnp.concatenate([right_all[t, k, 0], right_all[t, k, 1]], axis=1)
            term = jnp.dot(block, right_hot[k], preferred_element_type=F32) * off_diagonal(orb, k)
            right_part[t, 0] += term[:, :COLS]
            right_part[t, 1] += term[:, COLS:]

        def right_far():
            for copy in z_copies:
                copy.wait_recv()
            for place in (rights.at[orb, 1 - half], rights.at[other]):
                x_two.append([send(place, place, to) for to in x_tos])

        def right_one():
            right_add(other)
            for n, by in enumerate((-1, 1, 2)):
                x_one[n].wait_recv()
                x_two[0][n].wait_recv()
                right_add(turn(x, by, NX) * 2 + b2)

        right_copy = []

        def right_two():
            for n, by in enumerate((-1, 1, 2)):
                x_two[1][n].wait_recv()
                right_add(turn(x, by, NX) * 2 + 1 - b2)
            right_recv[t, half] = right_part[t, half]
            right_copy.append(send(right_part.at[t, 1 - half], right_recv.at[t, half], half_pair))

        def nothing():
            pass

        panel_gather(
            lambda k, p, i: lefts.at[k, p, pl.ds(i * (ROWS // 2), ROWS // 2)],
            tuple(two(f, hook(t, i) if i else nothing) for i, f in enumerate((first, nothing, right_far, nothing, right_one, nothing, right_two, nothing))),
            left_add,
        )
        sib_copy = send(left_part.at[t, 1 - core], left_sib.at[t], sibling)
        hook(t, 8)()
        right_copy[0].wait_recv()
        right_term = right_recv[t].reshape(ROWS, COLS)
        sib_copy.wait_recv()
        left_term = left_part[t, core] + left_sib[t]
        return weight * ((left_term + right_term - exch[...].astype(F32)) / acc[:ROWS, :COLS])

    def start_fitted():
        hook(0, 0)()
        own_fit.start()
        acc[:ROWS, :COLS] = prepare()

    weight = listed()
    loads[0].wait()
    current = iteration(0, amps[...], start_fitted)
    hook(0, 9)()
    current = iteration(1, current, hook(1, 0))

    mir_sites = sites[0]
    sites[0] += 2
    mir_copies = []
    for t in range(2):
        mir_send[t] = current[:, t * ROWS : (t + 1) * ROWS].T
        mir_copies.append(
            pltpu.make_async_remote_copy(
                src_ref=mir_send.at[t], dst_ref=mir_recv.at[core],
                send_sem=send_sems.at[mir_sites + t], recv_sem=recv_sems.at[mir_sites + core],
                device_id=mirror[t], device_id_type=MESH,
            )
        )

        @pl.when(jnp.logical_not(mine[t]))
        def _():
            mir_copies[t].start()

        @pl.when(mine[t])
        def _():
            mir_recv[t] = mir_send[t]

    hook(2, 0)()
    for t in range(2):

        @pl.when(jnp.logical_not(mine[t]))
        def _():
            pltpu.make_async_remote_copy(
                src_ref=mir_send.at[t], dst_ref=mir_recv.at[t],
                send_sem=send_sems.at[mir_sites + t], recv_sem=recv_sems.at[mir_sites + t],
                device_id=mirror[t], device_id_type=MESH,
            ).wait_recv()

    sym_halves = [
        0.5 * (current[:, t * ROWS : (t + 1) * ROWS] + mir_recv[t]) for t in range(2)
    ]
    for t in range(2):
        sym_out[:, t * ROWS : (t + 1) * ROWS] = sym_halves[t]
        sym_all[y, core, zl, t * ROWS : (t + 1) * ROWS] = sym_halves[t].T.astype(BF16)

    sib_copies = []

    def forward(k, distance):
        blocks = sym_all.at[k, core]
        sib_copies.append((k, send(blocks, blocks, sibling)))

    def nothing():
        pass

    panel_gather(
        lambda k, p, i: sym_all.at[k, core, p, pl.ds(i * ROWS, ROWS)],
        tuple(hook(3, i) for i in range(8)),
        forward,
    )
    own_fit.wait()
    for d in (0, -1, 1, 2):
        for n in range(COLS // PIECE):
            fit_last(d, n)
    acc[...] = jnp.zeros(acc.shape, F32)
    for k, copy in sib_copies:
        copy.wait_recv()
        panel = jnp.concatenate(
            [sym_all[k, 0, 0], sym_all[k, 1, 0], sym_all[k, 0, 1], sym_all[k, 1, 1]], axis=1
        )
        right = jnp.concatenate([fit_all[k * 2], fit_all[k * 2 + 1]], axis=0)
        acc[...] += jnp.dot(panel, right, preferred_element_type=F32)
    gamma_out[...] = acc[...].astype(BF16)

    for copy in sent:
        copy.wait_send()
    for t in range(2):

        @pl.when(jnp.logical_not(mine[t]))
        def _():
            mir_copies[t].wait_send()


def body(start_amps, exchange_ints, fitted_ints, pao_energy, occ_fock, domains, pair_list):
    vmem = pl.BlockSpec(memory_space=pltpu.VMEM)
    smem = pl.BlockSpec(memory_space=pltpu.SMEM)
    hbm = pl.BlockSpec(memory_space=pl.ANY)
    width = fitted_ints.shape[1]
    return pl.pallas_call(
        kernel,
        out_shape=(
            jax.ShapeDtypeStruct((ROWS, COLS), F32),
            jax.ShapeDtypeStruct((COLS, width), BF16),
        ),
        in_specs=[hbm, hbm, hbm, hbm, smem, hbm, smem],
        out_specs=(vmem, vmem),
        scratch_shapes=[
            pltpu.VMEM((NX * NZ, COLS, width), BF16),
            pltpu.VMEM((ITERS, NORB, 2, ROWS, COLS), BF16),
            pltpu.VMEM((ITERS, 2, HALF, COLS), BF16),
            pltpu.VMEM((ITERS, NORB, 2, HALF, COLS), BF16),
            pltpu.VMEM((ITERS, 2, ROWS, COLS), F32),
            pltpu.VMEM((ITERS, ROWS, COLS), F32),
            pltpu.VMEM((ITERS, 2, HALF, COLS), F32),
            pltpu.VMEM((ITERS, 2, HALF, COLS), F32),
            pltpu.VMEM((NORB, 2 * ROWS, 2 * ROWS), BF16),
            pltpu.VMEM((NORB, DOM, DOM), BF16),
            pltpu.VMEM((4, DOM, 1), F32),
            pltpu.VMEM((2, ROWS, ROWS), F32),
            pltpu.VMEM((2, ROWS, ROWS), F32),
            pltpu.VMEM((NY, 2, 2, COLS, ROWS), BF16),
            pltpu.VMEM((COLS, width), F32),
            pltpu.VMEM((ROWS, COLS), F32),
            pltpu.VMEM((ROWS, COLS), BF16),
            pltpu.VMEM((pao_energy.shape[0] // ROWS, ROWS), F32),
            pltpu.VMEM((NORB, DOM), jnp.int32),
            pltpu.SemaphoreType.DMA((MAX_COPIES,)),
            pltpu.SemaphoreType.DMA((MAX_COPIES,)),
            pltpu.SemaphoreType.DMA,
            pltpu.SemaphoreType.DMA((4,)),
        ],
        compiler_params=pltpu.CompilerParams(
            collective_id=0, has_side_effects=True, vmem_limit_bytes=60 * 1024 * 1024
        ),
        cost_estimate=pl.CostEstimate(flops=2_000_000_000, bytes_accessed=20_000_000, transcendentals=0),
    )(
        start_amps, exchange_ints, fitted_ints, pao_energy.reshape(-1, ROWS), occ_fock, domains, pair_list.T
    )


def solution(mesh):
    return jax.shard_map(
        body,
        mesh=mesh,
        in_specs=(P("row", "col"), P("row", "col"), P("col", "row"), P(), P(), P(), P()),
        out_specs=(P("row", "col"), P("col", "row")),
        check_vma=False,
    )
```

```python
import jax
import jax.numpy as jnp
from jax import lax
from jax.experimental import pallas as pl
from jax.experimental.pallas import tpu as pltpu
from jax.sharding import PartitionSpec as P

ITERS = 2
MESH = pl.DeviceIdType.MESH
F32 = jnp.float32
BF16 = jnp.bfloat16
ROWS, HALF, COLS, DOM, NORB = 128, 64, 256, 512, 8
NY, NX, NZ = 8, 4, 4
PIECES = ((0, 128, 'z'), (128, 96, 'z'), (224, 32, 'x'))
PLAN = {
    (0, 0): (('own', 0), ('trail', 0, 0)),
    (0, 2): (('own', 1),),
    (0, 4): (('trail', 0, 1), ('own', 2)),
    (0, 7): (('near', 0), ('near', 1), ('trail', 0, 2)),
    (0, 8): (('turn', 0, 0), ('turn', 0, 1)),
    (0, 9): (('trail', -1, 0), ('trail', -1, 1), ('near', 2)),
    (1, 2): (('trail', -1, 2), ('trail', 1, 2)),
    (1, 4): (('far', 0), ('far', 1), ('far', 2)),
    (1, 5): (('trail', 1, 0), ('trail', 1, 1)),
    (1, 7): (('turn', 0, 2), ('trail', 2, 2)),
    (1, 8): (('turn', -1, 0), ('turn', -1, 1)),
    (2, 0): (('trail', 2, 0), ('trail', 2, 1), ('turn', 1, 0), ('turn', 1, 1), ('turn', -1, 2), ('turn', 1, 2)),
    (3, 4): (('turn', 2, 0), ('turn', 2, 1), ('turn', 2, 2)),
}
MAX_COPIES = 256


def turn(place, by, count):
    return lax.rem(place + (by + count), count)


def kernel(
    amps_hbm, exch_hbm, fitted, energy_hbm, fock, dom_hbm, pairs,
    sym_out, gamma_out,
    fit_all, left_all, right_send, right_all, left_part, left_sib, right_part, right_recv,
    left_hot, right_hot, levels, mir_send, mir_relay, mir_recv, sym_all, acc, amps, exch, energy, dom,
    send_sems, recv_sems, own_sem, load_sems,
):
    row = lax.axis_index("row")
    col = lax.axis_index("col")
    y, quarter = row // 4, lax.rem(row, 4)
    zl, core = quarter // 2, lax.rem(quarter, 2)
    x, zh = col // 4, lax.rem(col, 4)
    b2, half = zh // 2, lax.rem(zh, 2)
    orb = col // 2

    def device(y_=y, zl_=zl, core_=core, x_=x, zh_=zh):
        return {"row": y_ * 4 + zl_ * 2 + core_, "col": x_ * 4 + zh_}

    y_up, y_down = device(y_=turn(y, 1, NY)), device(y_=turn(y, -1, NY))
    x_far = device(x_=turn(x, 2, NX))
    x_up, x_down = device(x_=turn(x, 1, NX)), device(x_=turn(x, -1, NX))
    z_up, z_down = device(zh_=turn(zh, 1, NZ)), device(zh_=turn(zh, -1, NZ))
    z_far = device(zh_=turn(zh, 2, NZ))
    z_other = device(zh_=(1 - b2) * 2 + 1 - half)
    z_pair = device(zl_=1 - zl)
    sibling = device(core_=1 - core)
    half_pair = device(zh_=b2 * 2 + 1 - half)
    diagonal = row // 2 == col
    relays = [
        {"row": col * 2 + c, "col": turn(row // 8, k, NX) * 4 + lax.rem(row // 2, 4)}
        for k in range(NX) for c in range(2)
    ]
    x_shares = [device(x_=turn(x, k, NX)) for k in range(1, NX)]
    mine = [jnp.logical_and(diagonal, core == t) for t in range(2)]

    loads = [
        pltpu.make_async_copy(src, dst, load_sems.at[n])
        for n, (src, dst) in enumerate(
            ((amps_hbm, amps), (dom_hbm, dom), (energy_hbm, energy), (exch_hbm, exch))
        )
    ]
    for load in loads:
        load.start()
    barrier = pltpu.get_barrier_semaphore()
    partners = [y_up, y_down, x_up, x_down, x_far, z_up, z_down, z_far, z_pair, sibling]
    for partner in partners + relays[2:]:
        pl.semaphore_signal(barrier, inc=1, device_id=partner, device_id_type=MESH)
    for c in range(2):

        @pl.when(jnp.logical_not(mine[c]))
        def _():
            pl.semaphore_signal(barrier, inc=1, device_id=relays[c], device_id_type=MESH)

    pl.semaphore_wait(barrier, len(partners) + 2 * NX - diagonal.astype(jnp.int32))

    sent = []
    sites = [0]

    def send(src, dst, target):
        site = sites[0]
        sites[0] += 1
        copy = pltpu.make_async_remote_copy(
            src_ref=src, dst_ref=dst, send_sem=send_sems.at[site], recv_sem=recv_sems.at[site],
            device_id=target, device_id_type=MESH,
        )
        copy.start()
        sent.append(copy)
        return copy

    fit_sent = {}

    def fit_ways(n, lead):
        along_z = (PIECES[n][2] == "z") == lead
        return (z_up, z_down) if along_z else (x_up, x_down)

    def fit_at(n, d, by=0, share=None):
        low, count, lead = PIECES[n]
        if share is not None:
            low, count = low + share * (count // 2), count // 2
        if lead == "x":
            d, by = by, d
        return fit_all.at[turn(x, by, NX) * NZ + turn(zh, d, NZ), pl.ds(low, count), :]

    def fit_mine(n):
        return fitted.at[pl.ds(PIECES[n][0], PIECES[n][1]), :]

    def fit_own(n):
        up, down = fit_ways(n, True)
        fit_sent["lead", -1, n] = send(fit_mine(n), fit_at(n, 0), up)
        fit_sent["lead", 1, n] = send(fit_mine(n), fit_at(n, 0), down)

    def fit_trail(d, n):
        src = fit_mine(n) if d == 0 else fit_at(n, d)
        fit_sent["trail", d, n] = [send(src, fit_at(n, d), to) for to in fit_ways(n, False)]

    def fit_near(n):
        for d, share, to in zip((-1, 1), (0, 1), fit_ways(n, True)):
            fit_sent["lead", d, n].wait_recv()
            block = fit_at(n, d, 0, share)
            fit_sent["far", share, n] = send(block, block, to)

    def fit_far(n):
        for share in range(2):
            fit_sent["far", share, n].wait_recv()

    def fit_turn(d, n):
        last = []
        for copy, by, share, to in zip(fit_sent["trail", d, n], (-1, 1), (0, 1), fit_ways(n, False)):
            copy.wait_recv()
            block = fit_at(n, d, by, share)
            last.append(send(block, block, to))
        fit_sent["last", d, n] = last

    def fit_last(d, n):
        for copy in fit_sent["last", d, n]:
            copy.wait_recv()

    actions = {
        "own": fit_own, "near": fit_near, "far": fit_far, "trail": fit_trail, "turn": fit_turn,
    }

    def hook(*place):
        def run():
            for step in PLAN.get(place, ()):
                actions[step[0]](*step[1:])

        return run

    own_fit = pltpu.make_async_copy(fitted, fit_all.at[col], own_sem)

    def listed():
        found = jnp.zeros((), jnp.bool_)
        for p in range(pairs.shape[1]):
            found = found | ((pairs[0, p] == y) & (pairs[1, p] == orb))
        return jnp.where(found, 1.0, 0.0)

    def off_diagonal(own, k):
        return jnp.where(own == k, 0.0, fock[own, k])

    def prepare():
        for load in loads[1:]:
            load.wait()
        domains = dom[...].astype(F32)
        columns = jnp.concatenate([domains, jnp.zeros((ROWS - NORB, DOM), F32)], axis=0).T
        lanes = lax.broadcasted_iota(jnp.int32, (DOM, ROWS), 1)

        def column_of(k):
            return jnp.sum(jnp.where(lanes == k, columns, 0.0), axis=1, keepdims=True)

        levels[2] = column_of(y)
        levels[3] = column_of(orb)
        own_rows = levels[2, pl.ds(pl.multiple_of(zl * 2 * ROWS, 2 * ROWS), 2 * ROWS), :]
        own_cols = dom[pl.ds(orb, 1), :].astype(F32)
        for k in range(NORB):
            picked = [
                dom[k : k + 1, pl.ds(pl.multiple_of((p * 2 + core) * ROWS, ROWS), ROWS)] for p in range(2)
            ]
            picked = jnp.concatenate(picked, axis=1).astype(F32)
            left_hot[k] = jnp.where(own_rows == picked, 1.0, 0.0).astype(BF16)
            right_hot[k] = jnp.where(columns[:, k : k + 1] == own_cols, 1.0, 0.0).astype(BF16)

        def level_of(paos):
            found = jnp.zeros((paos.shape[0], ROWS), F32)
            lane = lax.broadcasted_iota(jnp.int32, found.shape, 1).astype(F32)
            for r in range(energy.shape[0]):
                found += jnp.where(paos == lane + r * ROWS, energy[r : r + 1, :], 0.0)
            return jnp.sum(found, axis=1, keepdims=True)

        row_paos = levels[2, pl.ds(pl.multiple_of(quarter * ROWS, ROWS), ROWS), :]
        col_paos = levels[3, pl.ds(pl.multiple_of(half * COLS, COLS), COLS), :]
        row_level = level_of(row_paos) - fock[y, y]
        col_level = level_of(col_paos) - fock[orb, orb]
        return jnp.broadcast_to(row_level, (ROWS, COLS)) + jnp.broadcast_to(col_level, (COLS, ROWS)).T

    def panel_gather(at, between, arrived):
        parts = range(2)
        streams = [(zl, i) for i in parts] + [(1 - zl, i) for i in parts]
        pairs_in = [send(at(y, *at_), at(y, *at_), z_pair) for at_ in streams[:2]]
        ups = [send(at(y, *at_), at(y, *at_), y_up) for at_ in streams[:2]]
        downs = [send(at(y, *at_), at(y, *at_), y_down) for at_ in streams[:2]]
        between[0]()
        for copy, at_ in zip(pairs_in, streams[2:]):
            copy.wait_recv()
            ups.append(send(at(y, *at_), at(y, *at_), y_up))
            downs.append(send(at(y, *at_), at(y, *at_), y_down))
        arrived(y, None)
        for distance in (1, 2, 3):
            below, above = turn(y, -distance, NY), turn(y, distance, NY)
            for n, at_ in enumerate(streams):
                ups[n].wait_recv()
                if distance < 3 or n < 2:
                    ups[n] = send(at(below, *at_), at(below, *at_), y_up)
                downs[n].wait_recv()
                if distance < 3 or n >= 2:
                    downs[n] = send(at(above, *at_), at(above, *at_), y_down)
                if n % 2 == 1:
                    between[distance * 2 - 1 + n // 2]()
            arrived(below, distance)
            arrived(above, distance)
        for n in range(4):
            (ups if n < 2 else downs)[n].wait_recv()
        arrived(turn(y, 4, NY), 4)
        between[7]()

    def two(f, g):
        def run():
            f()
            g()

        return run

    def iteration(t, current, first):
        rounded = current.astype(BF16)
        left_all[t, y, zl] = rounded
        right_send[t] = rounded.reshape(2, HALF, COLS)
        right_all[t, orb, half] = right_send[t, half]
        lefts, rights = left_all.at[t], right_all.at[t]
        other = x * 2 + 1 - b2
        sources = right_send.at[t]
        z_copies = [
            send(sources.at[1 - half], rights.at[orb, half], half_pair),
            send(sources.at[half], rights.at[orb, half], z_far),
            send(sources.at[1 - half], rights.at[orb, half], z_other),
        ]
        x_tos = (x_up, x_down, x_far)
        x_one = [send(rights.at[orb, half], rights.at[orb, half], to) for to in x_tos]
        x_two = []
        left_part[t] = jnp.zeros((2, ROWS, COLS), F32)
        right_part[t] = jnp.zeros((2, HALF, COLS), F32)

        def left_add(k, distance):
            if distance is not None:
                block = left_all[t, k].reshape(2 * ROWS, COLS)
                term = jnp.dot(left_hot[k], block, preferred_element_type=F32) * off_diagonal(y, k)
                left_part[t] += term.reshape(2, ROWS, COLS)

        def right_add(k):
            block = jnp.concatenate([right_all[t, k, 0], right_all[t, k, 1]], axis=1)
            term = jnp.dot(block, right_hot[k], preferred_element_type=F32) * off_diagonal(orb, k)
            right_part[t, 0] += term[:, :COLS]
            right_part[t, 1] += term[:, COLS:]

        def right_far():
            for copy in z_copies:
                copy.wait_recv()
            for place in (rights.at[orb, 1 - half], rights.at[other]):
                x_two.append([send(place, place, to) for to in x_tos])

        def right_one():
            right_add(other)
            for n, by in enumerate((-1, 1, 2)):
                x_one[n].wait_recv()
                x_two[0][n].wait_recv()
                right_add(turn(x, by, NX) * 2 + b2)

        right_copy = []

        def right_two():
            for n, by in enumerate((-1, 1, 2)):
                x_two[1][n].wait_recv()
                right_add(turn(x, by, NX) * 2 + 1 - b2)
            right_recv[t, half] = right_part[t, half]
            right_copy.append(send(right_part.at[t, 1 - half], right_recv.at[t, half], half_pair))

        def nothing():
            pass

        panel_gather(
            lambda k, p, i: lefts.at[k, p, pl.ds(i * (ROWS // 2), ROWS // 2)],
            tuple(two(f, hook(t, i) if i else nothing) for i, f in enumerate((first, nothing, right_far, nothing, right_one, nothing, right_two, nothing))),
            left_add,
        )
        sib_copy = send(left_part.at[t, 1 - core], left_sib.at[t], sibling)
        hook(t, 8)()
        right_copy[0].wait_recv()
        right_term = right_recv[t].reshape(ROWS, COLS)
        sib_copy.wait_recv()
        left_term = left_part[t, core] + left_sib[t]
        return weight * ((left_term + right_term - exch[...].astype(F32)) / acc[:ROWS, :COLS])

    def start_fitted():
        hook(0, 0)()
        own_fit.start()
        acc[:ROWS, :COLS] = prepare()

    weight = listed()
    loads[0].wait()
    current = iteration(0, amps[...], start_fitted)
    hook(0, 9)()
    current = iteration(1, current, hook(1, 0))

    mir_sites = sites[0]
    sites[0] += 2 * NX
    mir_rows = ROWS // NX
    for t in range(2):
        tile = current[:, t * ROWS : (t + 1) * ROWS].T
        for k in range(NX):
            mir_send[k, t] = tile[k * mir_rows : (k + 1) * mir_rows]
    shared = [
        send(mir_send.at[k], mir_relay.at[k], x_shares[k - 1]) for k in range(1, NX)
    ]

    def mirror_copy(k, t):
        source = mir_send if k == 0 else mir_relay
        return pltpu.make_async_remote_copy(
            src_ref=source.at[k, t], dst_ref=mir_recv.at[core, pl.ds(k * mir_rows, mir_rows)],
            send_sem=send_sems.at[mir_sites + k * 2 + t],
            recv_sem=recv_sems.at[mir_sites + core * NX + k],
            device_id={"row": (turn(x, -k, NX) * 4 + zh) * 2 + t, "col": row // 2}, device_id_type=MESH,
        )

    for t in range(2):

        @pl.when(jnp.logical_not(mine[t]))
        def _():
            mirror_copy(0, t).start()

        @pl.when(mine[t])
        def _():
            pltpu.make_async_copy(
                mir_send.at[0, t], mir_recv.at[core, pl.ds(0, mir_rows)],
                recv_sems.at[mir_sites + core * NX],
            ).start()

    for k in range(1, NX):
        shared[k - 1].wait_recv()
        for t in range(2):
            copy = mirror_copy(k, t)
            copy.start()
            sent.append(copy)
    hook(2, 0)()
    for c in range(2):
        for k in range(NX):
            place = mir_recv.at[c, pl.ds(k * mir_rows, mir_rows)]
            pltpu.make_async_copy(place, place, recv_sems.at[mir_sites + c * NX + k]).wait()

    sym_halves = [
        0.5 * (current[:, t * ROWS : (t + 1) * ROWS] + mir_recv[t]) for t in range(2)
    ]
    for t in range(2):
        sym_out[:, t * ROWS : (t + 1) * ROWS] = sym_halves[t]
        sym_all[y, core, zl, t * ROWS : (t + 1) * ROWS] = sym_halves[t].T.astype(BF16)

    sib_copies = []

    def forward(k, distance):
        blocks = sym_all.at[k, core]
        sib_copies.append((k, send(blocks, blocks, sibling)))

    def nothing():
        pass

    panel_gather(
        lambda k, p, i: sym_all.at[k, core, p, pl.ds(i * ROWS, ROWS)],
        tuple(hook(3, i) for i in range(8)),
        forward,
    )
    own_fit.wait()
    for d in (0, -1, 1, 2):
        for n in range(len(PIECES)):
            fit_last(d, n)
    acc[...] = jnp.zeros(acc.shape, F32)
    for k, copy in sib_copies:
        copy.wait_recv()
        panel = jnp.concatenate(
            [sym_all[k, 0, 0], sym_all[k, 1, 0], sym_all[k, 0, 1], sym_all[k, 1, 1]], axis=1
        )
        right = jnp.concatenate([fit_all[k * 2], fit_all[k * 2 + 1]], axis=0)
        acc[...] += jnp.dot(panel, right, preferred_element_type=F32)
    gamma_out[...] = acc[...].astype(BF16)

    for copy in sent:
        copy.wait_send()
    for t in range(2):

        @pl.when(jnp.logical_not(mine[t]))
        def _():
            mirror_copy(0, t).wait_send()


def in_hbm(array):
    return pltpu.with_memory_space_constraint(array, pltpu.HBM)


def body(start_amps, exchange_ints, fitted_ints, pao_energy, occ_fock, domains, pair_list):
    vmem = pl.BlockSpec(memory_space=pltpu.VMEM)
    smem = pl.BlockSpec(memory_space=pltpu.SMEM)
    hbm = pl.BlockSpec(memory_space=pl.ANY)
    width = fitted_ints.shape[1]
    return pl.pallas_call(
        kernel,
        out_shape=(
            jax.ShapeDtypeStruct((ROWS, COLS), F32),
            jax.ShapeDtypeStruct((COLS, width), BF16),
        ),
        in_specs=[hbm, hbm, hbm, hbm, smem, hbm, smem],
        out_specs=(vmem, vmem),
        scratch_shapes=[
            pltpu.VMEM((NX * NZ, COLS, width), BF16),
            pltpu.VMEM((ITERS, NORB, 2, ROWS, COLS), BF16),
            pltpu.VMEM((ITERS, 2, HALF, COLS), BF16),
            pltpu.VMEM((ITERS, NORB, 2, HALF, COLS), BF16),
            pltpu.VMEM((ITERS, 2, ROWS, COLS), F32),
            pltpu.VMEM((ITERS, ROWS, COLS), F32),
            pltpu.VMEM((ITERS, 2, HALF, COLS), F32),
            pltpu.VMEM((ITERS, 2, HALF, COLS), F32),
            pltpu.VMEM((NORB, 2 * ROWS, 2 * ROWS), BF16),
            pltpu.VMEM((NORB, DOM, DOM), BF16),
            pltpu.VMEM((4, DOM, 1), F32),
            pltpu.VMEM((NX, 2, ROWS // NX, ROWS), F32),
            pltpu.VMEM((NX, 2, ROWS // NX, ROWS), F32),
            pltpu.VMEM((2, ROWS, ROWS), F32),
            pltpu.VMEM((NY, 2, 2, COLS, ROWS), BF16),
            pltpu.VMEM((COLS, width), F32),
            pltpu.VMEM((ROWS, COLS), F32),
            pltpu.VMEM((ROWS, COLS), BF16),
            pltpu.VMEM((pao_energy.shape[0] // ROWS, ROWS), F32),
            pltpu.VMEM((NORB, DOM), jnp.int32),
            pltpu.SemaphoreType.DMA((MAX_COPIES,)),
            pltpu.SemaphoreType.DMA((MAX_COPIES,)),
            pltpu.SemaphoreType.DMA,
            pltpu.SemaphoreType.DMA((4,)),
        ],
        compiler_params=pltpu.CompilerParams(
            collective_id=0, has_side_effects=True, vmem_limit_bytes=48 * 1024 * 1024
        ),
        cost_estimate=pl.CostEstimate(flops=2_000_000_000, bytes_accessed=20_000_000, transcendentals=0),
    )(
        in_hbm(start_amps), in_hbm(exchange_ints), in_hbm(fitted_ints), in_hbm(pao_energy.reshape(-1, ROWS)),
        in_hbm(occ_fock), in_hbm(domains), in_hbm(pair_list.T),
    )


def solution(mesh):
    return jax.shard_map(
        body,
        mesh=mesh,
        in_specs=(P("row", "col"), P("row", "col"), P("col", "row"), P(), P(), P(), P()),
        out_specs=(P("row", "col"), P("col", "row")),
        check_vma=False,
    )
```

```python
import jax
import jax.numpy as jnp
from jax import lax
from jax.experimental import pallas as pl
from jax.experimental.pallas import tpu as pltpu
from jax.sharding import PartitionSpec as P

ITERS = 2
MESH = pl.DeviceIdType.MESH
F32 = jnp.float32
BF16 = jnp.bfloat16
ROWS, HALF, COLS, DOM, NORB = 128, 64, 256, 512, 8
NY, NX, NZ = 8, 4, 4
PIECES = ((0, 128, 'z'), (128, 96, 'z'), (224, 32, 'x'))
PLAN = {
    (0, 0): (('own', 0), ('trail', 0, 0)),
    (0, 2): (('own', 1),),
    (0, 4): (('trail', 0, 1), ('own', 2)),
    (0, 8): (('near', 0), ('near', 1), ('trail', 0, 2), ('turn', 0, 0), ('turn', 0, 1)),
    (1, 0): (('trail', -1, 0), ('trail', -1, 1), ('near', 2)),
    (1, 2): (('trail', -1, 2), ('trail', 1, 2)),
    (1, 4): (('far', 0), ('far', 1), ('far', 2)),
    (1, 5): (('trail', 1, 0), ('trail', 1, 1)),
    (1, 8): (('turn', 0, 2), ('trail', 2, 2), ('turn', -1, 0), ('turn', -1, 1)),
    (2, 0): (('trail', 2, 0), ('trail', 2, 1), ('turn', 1, 0), ('turn', 1, 1), ('turn', -1, 2), ('turn', 1, 2)),
    (3, 4): (('turn', 2, 0), ('turn', 2, 1), ('turn', 2, 2)),
}
MAX_COPIES = 256


def turn(place, by, count):
    return lax.rem(place + (by + count), count)


def kernel(
    amps_hbm, exch_hbm, fitted, energy_hbm, fock, dom_hbm, pairs,
    sym_out, gamma_out,
    fit_all, left_all, right_send, right_all, left_part, left_sib, right_part, right_recv,
    left_hot, right_hot, levels, mir_send, mir_relay, mir_recv, sym_all, acc, amps, exch, energy, dom,
    send_sems, recv_sems, own_sem, load_sems,
):
    row = lax.axis_index("row")
    col = lax.axis_index("col")
    y, quarter = row // 4, lax.rem(row, 4)
    zl, core = quarter // 2, lax.rem(quarter, 2)
    x, zh = col // 4, lax.rem(col, 4)
    b2, half = zh // 2, lax.rem(zh, 2)
    orb = col // 2

    def device(y_=y, zl_=zl, core_=core, x_=x, zh_=zh):
        return {"row": y_ * 4 + zl_ * 2 + core_, "col": x_ * 4 + zh_}

    y_up, y_down = device(y_=turn(y, 1, NY)), device(y_=turn(y, -1, NY))
    x_far = device(x_=turn(x, 2, NX))
    x_up, x_down = device(x_=turn(x, 1, NX)), device(x_=turn(x, -1, NX))
    z_up, z_down = device(zh_=turn(zh, 1, NZ)), device(zh_=turn(zh, -1, NZ))
    z_far = device(zh_=turn(zh, 2, NZ))
    z_other = device(zh_=(1 - b2) * 2 + 1 - half)
    z_pair = device(zl_=1 - zl)
    sibling = device(core_=1 - core)
    half_pair = device(zh_=b2 * 2 + 1 - half)
    diagonal = row // 2 == col
    relays = [
        {"row": col * 2 + c, "col": turn(row // 8, k, NX) * 4 + lax.rem(row // 2, 4)}
        for k in range(NX) for c in range(2)
    ]
    x_shares = [device(x_=turn(x, k, NX)) for k in range(1, NX)]
    mine = [jnp.logical_and(diagonal, core == t) for t in range(2)]

    loads = [
        pltpu.make_async_copy(src, dst, load_sems.at[n])
        for n, (src, dst) in enumerate(
            ((amps_hbm, amps), (dom_hbm, dom), (energy_hbm, energy), (exch_hbm, exch))
        )
    ]
    for load in loads:
        load.start()
    barrier = pltpu.get_barrier_semaphore()
    partners = [y_up, y_down, x_up, x_down, x_far, z_up, z_down, z_far, z_pair, sibling]
    for partner in partners + relays[2:]:
        pl.semaphore_signal(barrier, inc=1, device_id=partner, device_id_type=MESH)
    for c in range(2):

        @pl.when(jnp.logical_not(mine[c]))
        def _():
            pl.semaphore_signal(barrier, inc=1, device_id=relays[c], device_id_type=MESH)

    pl.semaphore_wait(barrier, len(partners) + 2 * NX - diagonal.astype(jnp.int32))

    sent = []
    sites = [0]

    def send(src, dst, target):
        site = sites[0]
        sites[0] += 1
        copy = pltpu.make_async_remote_copy(
            src_ref=src, dst_ref=dst, send_sem=send_sems.at[site], recv_sem=recv_sems.at[site],
            device_id=target, device_id_type=MESH,
        )
        copy.start()
        sent.append(copy)
        return copy

    fit_sent = {}

    def fit_ways(n, lead):
        along_z = (PIECES[n][2] == "z") == lead
        return (z_up, z_down) if along_z else (x_up, x_down)

    def fit_at(n, d, by=0, share=None):
        low, count, lead = PIECES[n]
        if share is not None:
            low, count = low + share * (count // 2), count // 2
        if lead == "x":
            d, by = by, d
        return fit_all.at[turn(x, by, NX) * NZ + turn(zh, d, NZ), pl.ds(low, count), :]

    def fit_mine(n):
        return fitted.at[pl.ds(PIECES[n][0], PIECES[n][1]), :]

    def fit_own(n):
        up, down = fit_ways(n, True)
        fit_sent["lead", -1, n] = send(fit_mine(n), fit_at(n, 0), up)
        fit_sent["lead", 1, n] = send(fit_mine(n), fit_at(n, 0), down)

    def fit_trail(d, n):
        src = fit_mine(n) if d == 0 else fit_at(n, d)
        fit_sent["trail", d, n] = [send(src, fit_at(n, d), to) for to in fit_ways(n, False)]

    def fit_near(n):
        for d, share, to in zip((-1, 1), (0, 1), fit_ways(n, True)):
            fit_sent["lead", d, n].wait_recv()
            block = fit_at(n, d, 0, share)
            fit_sent["far", share, n] = send(block, block, to)

    def fit_far(n):
        for share in range(2):
            fit_sent["far", share, n].wait_recv()

    def fit_turn(d, n):
        last = []
        for copy, by, share, to in zip(fit_sent["trail", d, n], (-1, 1), (0, 1), fit_ways(n, False)):
            copy.wait_recv()
            block = fit_at(n, d, by, share)
            last.append(send(block, block, to))
        fit_sent["last", d, n] = last

    def fit_last(d, n):
        for copy in fit_sent["last", d, n]:
            copy.wait_recv()

    actions = {
        "own": fit_own, "near": fit_near, "far": fit_far, "trail": fit_trail, "turn": fit_turn,
    }

    def hook(*place):
        def run():
            for step in PLAN.get(place, ()):
                actions[step[0]](*step[1:])

        return run

    own_fit = pltpu.make_async_copy(fitted, fit_all.at[col], own_sem)

    def listed():
        found = jnp.zeros((), jnp.bool_)
        for p in range(pairs.shape[1]):
            found = found | ((pairs[0, p] == y) & (pairs[1, p] == orb))
        return jnp.where(found, 1.0, 0.0)

    def off_diagonal(own, k):
        return jnp.where(own == k, 0.0, fock[own, k])

    def prepare():
        for load in loads[1:]:
            load.wait()
        domains = dom[...].astype(F32)
        columns = jnp.concatenate([domains, jnp.zeros((ROWS - NORB, DOM), F32)], axis=0).T
        lanes = lax.broadcasted_iota(jnp.int32, (DOM, ROWS), 1)

        def column_of(k):
            return jnp.sum(jnp.where(lanes == k, columns, 0.0), axis=1, keepdims=True)

        levels[2] = column_of(y)
        levels[3] = column_of(orb)
        own_rows = levels[2, pl.ds(pl.multiple_of(zl * 2 * ROWS, 2 * ROWS), 2 * ROWS), :]
        own_cols = dom[pl.ds(orb, 1), :].astype(F32)
        for k in range(NORB):
            picked = [
                dom[k : k + 1, pl.ds(pl.multiple_of((p * 2 + core) * ROWS, ROWS), ROWS)] for p in range(2)
            ]
            picked = jnp.concatenate(picked, axis=1).astype(F32)
            left_hot[k] = jnp.where(own_rows == picked, 1.0, 0.0).astype(BF16)
            right_hot[k] = jnp.where(columns[:, k : k + 1] == own_cols, 1.0, 0.0).astype(BF16)

        def level_of(paos):
            found = jnp.zeros((paos.shape[0], ROWS), F32)
            lane = lax.broadcasted_iota(jnp.int32, found.shape, 1).astype(F32)
            for r in range(energy.shape[0]):
                found += jnp.where(paos == lane + r * ROWS, energy[r : r + 1, :], 0.0)
            return jnp.sum(found, axis=1, keepdims=True)

        row_paos = levels[2, pl.ds(pl.multiple_of(quarter * ROWS, ROWS), ROWS), :]
        col_paos = levels[3, pl.ds(pl.multiple_of(half * COLS, COLS), COLS), :]
        row_level = level_of(row_paos) - fock[y, y]
        col_level = level_of(col_paos) - fock[orb, orb]
        return jnp.broadcast_to(row_level, (ROWS, COLS)) + jnp.broadcast_to(col_level, (COLS, ROWS)).T

    def panel_gather(at, between, arrived):
        parts = range(2)
        streams = [(zl, i) for i in parts] + [(1 - zl, i) for i in parts]
        pairs_in = [send(at(y, *at_), at(y, *at_), z_pair) for at_ in streams[:2]]
        ups = [send(at(y, *at_), at(y, *at_), y_up) for at_ in streams[:2]]
        downs = [send(at(y, *at_), at(y, *at_), y_down) for at_ in streams[:2]]
        between[0]()
        for copy, at_ in zip(pairs_in, streams[2:]):
            copy.wait_recv()
            ups.append(send(at(y, *at_), at(y, *at_), y_up))
            downs.append(send(at(y, *at_), at(y, *at_), y_down))
        arrived(y, None)
        for distance in (1, 2, 3):
            below, above = turn(y, -distance, NY), turn(y, distance, NY)
            for n, at_ in enumerate(streams):
                ups[n].wait_recv()
                if distance < 3 or n < 2:
                    ups[n] = send(at(below, *at_), at(below, *at_), y_up)
                downs[n].wait_recv()
                if distance < 3 or n >= 2:
                    downs[n] = send(at(above, *at_), at(above, *at_), y_down)
                if n % 2 == 1:
                    between[distance * 2 - 1 + n // 2]()
            arrived(below, distance)
            arrived(above, distance)
        for n in range(4):
            (ups if n < 2 else downs)[n].wait_recv()
        arrived(turn(y, 4, NY), 4)
        between[7]()

    def two(f, g):
        def run():
            f()
            g()

        return run

    def iteration(t, current, first):
        rounded = current.astype(BF16)
        left_all[t, y, zl] = rounded
        right_send[t] = rounded.reshape(2, HALF, COLS)
        right_all[t, orb, half] = right_send[t, half]
        lefts, rights = left_all.at[t], right_all.at[t]
        other = x * 2 + 1 - b2
        sources = right_send.at[t]
        z_copies = [
            send(sources.at[1 - half], rights.at[orb, half], half_pair),
            send(sources.at[half], rights.at[orb, half], z_far),
            send(sources.at[1 - half], rights.at[orb, half], z_other),
        ]
        x_tos = (x_up, x_down, x_far)
        x_one = [send(rights.at[orb, half], rights.at[orb, half], to) for to in x_tos]
        x_two = []
        left_part[t] = jnp.zeros((2, ROWS, COLS), F32)
        right_part[t] = jnp.zeros((2, HALF, COLS), F32)

        def left_add(k, distance):
            if distance is not None:
                block = left_all[t, k].reshape(2 * ROWS, COLS)
                term = jnp.dot(left_hot[k], block, preferred_element_type=F32) * off_diagonal(y, k)
                left_part[t] += term.reshape(2, ROWS, COLS)

        def right_add(k):
            block = jnp.concatenate([right_all[t, k, 0], right_all[t, k, 1]], axis=1)
            term = jnp.dot(block, right_hot[k], preferred_element_type=F32) * off_diagonal(orb, k)
            right_part[t, 0] += term[:, :COLS]
            right_part[t, 1] += term[:, COLS:]

        def right_far():
            for copy in z_copies:
                copy.wait_recv()
            for place in (rights.at[orb, 1 - half], rights.at[other]):
                x_two.append([send(place, place, to) for to in x_tos])

        def right_one():
            right_add(other)
            for n, by in enumerate((-1, 1, 2)):
                x_one[n].wait_recv()
                x_two[0][n].wait_recv()
                right_add(turn(x, by, NX) * 2 + b2)

        right_copy = []

        def right_two():
            for n, by in enumerate((-1, 1, 2)):
                x_two[1][n].wait_recv()
                right_add(turn(x, by, NX) * 2 + 1 - b2)
            right_recv[t, half] = right_part[t, half]
            right_copy.append(send(right_part.at[t, 1 - half], right_recv.at[t, half], half_pair))

        def nothing():
            pass

        panel_gather(
            lambda k, p, i: lefts.at[k, p, pl.ds(i * (ROWS // 2), ROWS // 2)],
            tuple(two(f, hook(t, i) if i else nothing) for i, f in enumerate((first, nothing, right_far, nothing, right_one, nothing, right_two, nothing))),
            left_add,
        )
        sib_copy = send(left_part.at[t, 1 - core], left_sib.at[t], sibling)
        hook(t, 8)()
        right_copy[0].wait_recv()
        right_term = right_recv[t].reshape(ROWS, COLS)
        sib_copy.wait_recv()
        left_term = left_part[t, core] + left_sib[t]
        return weight[0] * ((left_term + right_term - exch[...].astype(F32)) / acc[:ROWS, :COLS])

    weight = []

    def start_fitted():
        hook(0, 0)()
        own_fit.start()
        weight.append(listed())
        acc[:ROWS, :COLS] = prepare()

    loads[0].wait()
    current = iteration(0, amps[...], start_fitted)
    hook(0, 9)()
    current = iteration(1, current, hook(1, 0))

    mir_sites = sites[0]
    sites[0] += 2 * NX
    mir_rows = ROWS // NX
    for t in range(2):
        tile = current[:, t * ROWS : (t + 1) * ROWS].T
        for k in range(NX):
            mir_send[k, t] = tile[k * mir_rows : (k + 1) * mir_rows]
    shared = [
        send(mir_send.at[k], mir_relay.at[k], x_shares[k - 1]) for k in range(1, NX)
    ]

    def mirror_copy(k, t):
        source = mir_send if k == 0 else mir_relay
        return pltpu.make_async_remote_copy(
            src_ref=source.at[k, t], dst_ref=mir_recv.at[core, pl.ds(k * mir_rows, mir_rows)],
            send_sem=send_sems.at[mir_sites + k * 2 + t],
            recv_sem=recv_sems.at[mir_sites + core * NX + k],
            device_id={"row": (turn(x, -k, NX) * 4 + zh) * 2 + t, "col": row // 2}, device_id_type=MESH,
        )

    for t in range(2):

        @pl.when(jnp.logical_not(mine[t]))
        def _():
            mirror_copy(0, t).start()

        @pl.when(mine[t])
        def _():
            pltpu.make_async_copy(
                mir_send.at[0, t], mir_recv.at[core, pl.ds(0, mir_rows)],
                recv_sems.at[mir_sites + core * NX],
            ).start()

    for k in range(1, NX):
        shared[k - 1].wait_recv()
        for t in range(2):
            copy = mirror_copy(k, t)
            copy.start()
            sent.append(copy)
    hook(2, 0)()
    for c in range(2):
        for k in range(NX):
            place = mir_recv.at[c, pl.ds(k * mir_rows, mir_rows)]
            pltpu.make_async_copy(place, place, recv_sems.at[mir_sites + c * NX + k]).wait()

    sym_halves = [
        0.5 * (current[:, t * ROWS : (t + 1) * ROWS] + mir_recv[t]) for t in range(2)
    ]
    for t in range(2):
        sym_out[:, t * ROWS : (t + 1) * ROWS] = sym_halves[t]
        sym_all[y, core, zl, t * ROWS : (t + 1) * ROWS] = sym_halves[t].T.astype(BF16)

    sib_copies = []

    def forward(k, distance):
        blocks = sym_all.at[k, core]
        sib_copies.append((k, send(blocks, blocks, sibling)))

    def nothing():
        pass

    panel_gather(
        lambda k, p, i: sym_all.at[k, core, p, pl.ds(i * ROWS, ROWS)],
        tuple(hook(3, i) for i in range(8)),
        forward,
    )
    own_fit.wait()
    for d in (0, -1, 1, 2):
        for n in range(len(PIECES)):
            fit_last(d, n)
    acc[...] = jnp.zeros(acc.shape, F32)
    for k, copy in sib_copies:
        copy.wait_recv()
        panel = jnp.concatenate(
            [sym_all[k, 0, 0], sym_all[k, 1, 0], sym_all[k, 0, 1], sym_all[k, 1, 1]], axis=1
        )
        right = jnp.concatenate([fit_all[k * 2], fit_all[k * 2 + 1]], axis=0)
        acc[...] += jnp.dot(panel, right, preferred_element_type=F32)
    gamma_out[...] = acc[...].astype(BF16)

    for copy in sent:
        copy.wait_send()
    for t in range(2):

        @pl.when(jnp.logical_not(mine[t]))
        def _():
            mirror_copy(0, t).wait_send()


def in_hbm(array):
    return pltpu.with_memory_space_constraint(array, pltpu.HBM)


def body(start_amps, exchange_ints, fitted_ints, pao_energy, occ_fock, domains, pair_list):
    vmem = pl.BlockSpec(memory_space=pltpu.VMEM)
    smem = pl.BlockSpec(memory_space=pltpu.SMEM)
    hbm = pl.BlockSpec(memory_space=pl.ANY)
    width = fitted_ints.shape[1]
    return pl.pallas_call(
        kernel,
        out_shape=(
            jax.ShapeDtypeStruct((ROWS, COLS), F32),
            jax.ShapeDtypeStruct((COLS, width), BF16),
        ),
        in_specs=[hbm, hbm, hbm, hbm, smem, hbm, smem],
        out_specs=(vmem, vmem),
        scratch_shapes=[
            pltpu.VMEM((NX * NZ, COLS, width), BF16),
            pltpu.VMEM((ITERS, NORB, 2, ROWS, COLS), BF16),
            pltpu.VMEM((ITERS, 2, HALF, COLS), BF16),
            pltpu.VMEM((ITERS, NORB, 2, HALF, COLS), BF16),
            pltpu.VMEM((ITERS, 2, ROWS, COLS), F32),
            pltpu.VMEM((ITERS, ROWS, COLS), F32),
            pltpu.VMEM((ITERS, 2, HALF, COLS), F32),
            pltpu.VMEM((ITERS, 2, HALF, COLS), F32),
            pltpu.VMEM((NORB, 2 * ROWS, 2 * ROWS), BF16),
            pltpu.VMEM((NORB, DOM, DOM), BF16),
            pltpu.VMEM((4, DOM, 1), F32),
            pltpu.VMEM((NX, 2, ROWS // NX, ROWS), F32),
            pltpu.VMEM((NX, 2, ROWS // NX, ROWS), F32),
            pltpu.VMEM((2, ROWS, ROWS), F32),
            pltpu.VMEM((NY, 2, 2, COLS, ROWS), BF16),
            pltpu.VMEM((COLS, width), F32),
            pltpu.VMEM((ROWS, COLS), F32),
            pltpu.VMEM((ROWS, COLS), BF16),
            pltpu.VMEM((pao_energy.shape[0] // ROWS, ROWS), F32),
            pltpu.VMEM((NORB, DOM), jnp.int32),
            pltpu.SemaphoreType.DMA((MAX_COPIES,)),
            pltpu.SemaphoreType.DMA((MAX_COPIES,)),
            pltpu.SemaphoreType.DMA,
            pltpu.SemaphoreType.DMA((4,)),
        ],
        compiler_params=pltpu.CompilerParams(
            collective_id=0, has_side_effects=True, vmem_limit_bytes=48 * 1024 * 1024
        ),
        cost_estimate=pl.CostEstimate(flops=2_000_000_000, bytes_accessed=20_000_000, transcendentals=0),
    )(
        in_hbm(start_amps), in_hbm(exchange_ints), in_hbm(fitted_ints), in_hbm(pao_energy.reshape(-1, ROWS)),
        in_hbm(occ_fock), in_hbm(domains), in_hbm(pair_list.T),
    )


def solution(mesh):
    return jax.shard_map(
        body,
        mesh=mesh,
        in_specs=(P("row", "col"), P("row", "col"), P("col", "row"), P(), P(), P(), P()),
        out_specs=(P("row", "col"), P("col", "row")),
        check_vma=False,
    )
```
